512 devices in a mesh: hist: 16 (over z_hi, x, core), user: 32 (over z_lo, y).
Axes of the slice: x: 4, y: 4, z: 16 (z_hi: 2, z_lo: 8; z = z_hi * 8 + z_lo), core: 2. Of those that a mesh axis runs over, the one named last changes fastest.
Arguments:
- cand_embed: bfloat16 [32, 1024, 1024], P('user', 'hist'), may hold values from -6 to 6
- hist_key: bfloat16 [32, 4096, 1024], P('user', 'hist'), may hold values from -6 to 6
- hist_value: bfloat16 [32, 4096, 1024], P('user', 'hist'), may hold values from -6 to 6
- block_owner: int32 [32, 32], P('user'), may hold values from 0 to 3, as said below
- cand_user: int32 [32, 1024], P('user', 'hist'), may hold values from 0 to 3, as said below
- cand_cutoff: int32 [32, 1024], P('user', 'hist'), may hold values from 1 to 4096, as said below
- w_in: bfloat16 [1024, 4096], P('user'), may hold values from -0.1875 to 0.1875
- w_out: bfloat16 [1024, 1024], P('user'), may hold values from -0.1875 to 0.1875
Outputs:
- cand_out: bfloat16 [32, 1024, 1024], P('user', 'hist')
The draws below stay inside these ranges and needn't reach their ends.
Inputs may be any that keep to these rules, and one draw needn't show every extreme that they name: `block_owner`: in each group the owners never fall along the blocks, and each of the 4 users owns one or more blocks. `cand_user`: every user of a group has candidates. `cand_cutoff`: A candidate's cutoff lies after the first event of its user and not after the user's last event plus one.
All inputs are finite; a program needn't handle non-finite values.
Results may differ from the reference program's by a relative error of at most 0.0055.
Values may be sent and summed in bfloat16 or wider, within the bound.
No kernel may reach another device: no remote copies, remote signals or barrier semaphores. Data moves between devices by JAX's collectives and lax.ppermute only.
A program may use at most 64 MiB of HBM per device.

```python
import jax
import jax.numpy as jnp
from jax import lax

D = 1024
HEADS = 8
HEAD = 128
BLOCK = 128
USERS_GRP = 4
CAND_DEV = 64
GRP = 32
EVENTS_GRP = 4096
BLOCKS_GRP = 32
CAND_GRP = 1024
N_HIST = 16


def group_layout(key):
    key = jax.random.fold_in(key, 11)

    def one_group(group_key):
        cut_key, user_key, off_key = jax.random.split(group_key, 3)
        picks = jax.random.permutation(cut_key, BLOCKS_GRP - 1)[:USERS_GRP - 1] + 1
        cuts = jnp.sort(picks).astype(jnp.int32)
        blocks = jnp.arange(BLOCKS_GRP, dtype=jnp.int32)
        owner = jnp.sum((blocks[:, None] >= cuts[None, :]).astype(jnp.int32), axis=1)
        lower = jnp.concatenate([jnp.zeros((1,), jnp.int32), cuts]) * BLOCK
        upper = jnp.concatenate([cuts * BLOCK, jnp.full((1,), EVENTS_GRP, jnp.int32)])
        users = jax.random.randint(user_key, (CAND_GRP,), 0, USERS_GRP).astype(jnp.int32)
        users = users.at[0:USERS_GRP].set(jnp.arange(USERS_GRP, dtype=jnp.int32))
        start = lower[users]
        span = upper[users] - start
        offset = jax.random.randint(off_key, (CAND_GRP,), 0, 1 << 30).astype(jnp.int32) % span
        cutoffs = start + 1 + offset
        cutoffs = cutoffs.at[0].set(1)
        cutoffs = cutoffs.at[USERS_GRP - 1].set(EVENTS_GRP)
        return (owner, users, cutoffs)
    return jax.vmap(one_group)(jax.random.split(key, GRP))


def draw_block_owner(key, part):
    return group_layout(key)[0]


def draw_cand_user(key, part):
    return group_layout(key)[1]


def draw_cand_cutoff(key, part):
    return group_layout(key)[2]


def shard_levels(rng, dims, pieces, low, high):
    loudness, own = 1.0, jax.random.fold_in(rng, 6)
    for position, blocks in pieces:
        steps = jnp.exp(jax.random.uniform(jax.random.fold_in(own, position), (blocks,), jnp.float32, low / len(pieces), high / len(pieces)))
        loudness = loudness * jnp.repeat(steps, dims[position] // blocks).reshape([-1 if axis == position else 1 for axis in range(len(dims))])
    return loudness


def noise(stream_key, dims, width, most, shards=(), kind=jnp.bfloat16):
    result = width * jax.random.normal(stream_key, dims, jnp.float32)
    if shards:
        result = result * shard_levels(stream_key, dims, shards, -0.22, 0.18)
    return jnp.clip(result, -most, most).astype(kind)


def setup_inputs(seed: int = 0) -> dict:
    key_of = jax.random.split(jax.random.key(seed), 9)
    cand_embed = noise(key_of[0], (GRP, CAND_GRP, D), 1.0, 6.0, ((0, 32), (1, 16)))
    hist_key = noise(key_of[1], (GRP, EVENTS_GRP, D), 1.0, 6.0, ((0, 32), (1, 16)))
    hist_value = noise(key_of[2], (GRP, EVENTS_GRP, D), 1.0, 6.0, ((0, 32), (1, 16)))
    block_owner = draw_block_owner(jax.random.fold_in(key_of[8], 71), 0)
    cand_user = draw_cand_user(jax.random.fold_in(key_of[8], 71), 0)
    cand_cutoff = draw_cand_cutoff(jax.random.fold_in(key_of[8], 71), 0)
    w_in = noise(key_of[6], (D, 4 * D), D ** -0.5, 0.1875, ((0, 32),))
    w_out = noise(key_of[7], (D, D), D ** -0.5, 0.1875, ((0, 32),))
    return dict(cand_embed=cand_embed, hist_key=hist_key, hist_value=hist_value, block_owner=block_owner, cand_user=cand_user, cand_cutoff=cand_cutoff, w_in=w_in, w_out=w_out)


def layer_norm(values):
    mean = lax.optimization_barrier(jnp.mean(values, axis=-1, keepdims=True))
    centred = values - mean
    var = lax.optimization_barrier(jnp.mean(centred * centred, axis=-1, keepdims=True))
    return centred * lax.rsqrt(var + 1e-05)

def visible_count(owner, users, cutoffs):
    starts = jnp.arange(owner.shape[0], dtype=jnp.int32) * BLOCK
    inside = jnp.clip(cutoffs[:, None] - starts[None, :], 0, BLOCK)
    same = owner[None, :] == users[:, None]
    return lax.optimization_barrier(jnp.sum(jnp.where(same, inside, 0), axis=1)).astype(jnp.float32)

def pointwise(query, users, cutoffs, keys, values, event_owner, positions):
    rows = query.shape[0]
    count = keys.shape[0]
    mask = (event_owner[None, :] == users[:, None]) & (positions[None, :] < cutoffs[:, None])
    q_heads = query.reshape(rows, HEADS, HEAD).astype(jnp.float32)
    k_heads = keys.reshape(count, HEADS, HEAD).astype(jnp.float32)
    scores = jnp.einsum('chd,ehd->hce', q_heads, k_heads) * HEAD ** (-0.5)
    weight = (jax.nn.silu(scores) * mask[None, :, :]).astype(jnp.bfloat16)
    v_heads = values.reshape(count, HEADS, HEAD).astype(jnp.float32)
    summed = jnp.einsum('hce,ehd->chd', weight.astype(jnp.float32), v_heads)
    return summed.reshape(rows, HEADS * HEAD)

def finish(x, proj, hist_sum, count, w_out_rows):
    rows = x.shape[0]
    gate = proj[:, 0:D].astype(jnp.float32)
    val = proj[:, D:2 * D].astype(jnp.float32).reshape(rows, HEADS, HEAD)
    query = proj[:, 2 * D:3 * D].astype(jnp.float32).reshape(rows, HEADS, HEAD)
    key_self = proj[:, 3 * D:4 * D].astype(jnp.float32).reshape(rows, HEADS, HEAD)
    self_weight = jax.nn.silu(lax.optimization_barrier(jnp.sum(query * key_self, axis=-1)) * HEAD ** (-0.5))
    attended = (hist_sum.reshape(rows, HEADS, HEAD) + self_weight[:, :, None] * val) / (count[:, None, None] + 1.0)
    mixed = (layer_norm(attended).reshape(rows, D) * gate).astype(jnp.bfloat16)
    return mixed

def reference(cand_embed, hist_key, hist_value, block_owner, cand_user, cand_cutoff, w_in, w_out):

    def group(items):
        x, keys, values, owner, users, cutoffs = items
        normed = layer_norm(x.astype(jnp.float32)).astype(jnp.bfloat16)
        proj = jax.nn.silu(jnp.dot(normed, w_in, preferred_element_type=jnp.float32)).astype(jnp.bfloat16)
        count = visible_count(owner, users, cutoffs)
        event_owner = jnp.repeat(owner, BLOCK)
        positions = jnp.arange(EVENTS_GRP, dtype=jnp.int32)
        queries = proj[:, 2 * D:3 * D].reshape(N_HIST, CAND_DEV, D)

        def one_block(block_items):
            q_block, u_block, c_block = block_items
            return pointwise(q_block, u_block, c_block, keys, values, event_owner, positions)
        hist_sum = lax.map(one_block, (queries, users.reshape(N_HIST, CAND_DEV), cutoffs.reshape(N_HIST, CAND_DEV)))
        hist_sum = hist_sum.reshape(CAND_GRP, D)
        mixed = finish(x, proj, hist_sum, count, w_out)
        out = x.astype(jnp.float32) + jnp.dot(mixed, w_out, preferred_element_type=jnp.float32)
        return out.astype(jnp.bfloat16)
    return lax.map(group, (cand_embed, hist_key, hist_value, block_owner, cand_user, cand_cutoff))
```

```python
import jax
import jax.numpy as jnp
from jax import lax
from jax.experimental import pallas as pl
from jax.experimental.pallas import tpu as pltpu
from jax.sharding import Mesh, PartitionSpec as P

D = 1024
HEADS = 8
HEAD = 128
BLOCK = 128
ROWS = 64
HALF = 512
EVENTS = 2048
USER = ("zl", "y")
LOCAL = ("x", "c")
HIST = ("zh", "x", "c")
SCALE = HEAD ** (-0.5)


def silu(v):
    h = v * 0.5
    return h + h * jnp.tanh(h)


def layer_norm(values):
    mean = jnp.mean(values, axis=-1, keepdims=True)
    centred = values - mean
    var = jnp.mean(centred * centred, axis=-1, keepdims=True)
    return centred * lax.rsqrt(var + 1e-05)


def spread(value, axis, count):
    copies = jnp.broadcast_to(value[None], (count,) + value.shape)
    return lax.all_to_all(copies, axis, 0, 0, tiled=True)


def attend_kernel(q_ref, k_ref, v_ref, lo_ref, hi_ref, out_ref):
    tile, chunk = 128, 512

    def rows(i, carry):
        at = pl.ds(pl.multiple_of(i * tile, tile), tile)
        q = q_ref[at, :]
        lo = jnp.broadcast_to(lo_ref[at, :], (tile, chunk))
        hi = jnp.broadcast_to(hi_ref[at, :], (tile, chunk))
        total = jnp.zeros((tile, HEAD), jnp.float32)
        for e in range(EVENTS // chunk):
            span = pl.ds(e * chunk, chunk)
            s = lax.dot_general(
                q, k_ref[span, :], (((1,), (1,)), ((), ())), preferred_element_type=jnp.float32
            )
            h = s * (0.5 * SCALE)
            w = h + h * jnp.tanh(h)
            event = lax.broadcasted_iota(jnp.int32, (tile, chunk), 1) + e * chunk
            seen = (event >= lo) & (event < hi)
            w = jnp.where(seen, w, 0.0).astype(jnp.bfloat16)
            total = total + jnp.dot(w, v_ref[span, :], preferred_element_type=jnp.float32)
        out_ref[at, :] = total.astype(out_ref.dtype)
        return carry

    lax.fori_loop(0, q_ref.shape[0] // tile, rows, 0)


def attend(query, keys, values, lo, hi, dtype):
    rows = query.shape[0]
    vmem = pl.BlockSpec(memory_space=pltpu.VMEM)
    return pl.pallas_call(
        attend_kernel,
        out_shape=jax.ShapeDtypeStruct((rows, HEAD), dtype),
        in_specs=[vmem] * 5,
        out_specs=vmem,
        cost_estimate=pl.CostEstimate(
            flops=4 * rows * EVENTS * HEAD, bytes_accessed=1 << 21, transcendentals=rows * EVENTS
        ),
        compiler_params=pltpu.CompilerParams(vmem_limit_bytes=32 << 20),
    )(query, keys, values, lo, hi)


def body(cand_embed, hist_key, hist_value, block_owner, cand_user, cand_cutoff, w_in, w_out):
    x = cand_embed[0]
    head = lax.axis_index("x") * 2 + lax.axis_index("c")
    half = lax.axis_index("zh")

    normed = layer_norm(x.astype(jnp.float32)).astype(jnp.bfloat16)
    normed = normed.reshape(ROWS, 8, 4, 32).transpose(0, 2, 1, 3).reshape(ROWS, D)
    before = jnp.sum((block_owner[0][None, :] < cand_user[0][:, None]).astype(jnp.int32), axis=1)
    cutoff = cand_cutoff[0]
    labels = jnp.stack([before, cutoff // 64, cutoff % 64]).astype(jnp.bfloat16)
    labels = jnp.pad(labels, ((0, 5), (0, D - ROWS)))
    mine = jnp.concatenate([normed, labels])
    other = lax.ppermute(mine, "zh", [(0, 1), (1, 0)])

    cols = lax.dynamic_slice_in_dim(w_in.reshape(32, 4, HEADS, HEAD), head, 1, 2).reshape(32, 512)
    cols = jnp.concatenate([cols, lax.dynamic_slice_in_dim(w_out, head * HEAD, HEAD, 1)], axis=1)
    cols = spread(cols, "zl", 8).reshape(256, 640)
    cols = spread(cols, "y", 4).reshape(D, 640)
    w_out_all = spread(cols[:, 512:], LOCAL, 8)

    both = jnp.stack([mine, other])
    both = spread(both, LOCAL, 8)
    normed_own = both[:, 0, :ROWS].reshape(HALF, D)
    normed_other = both[:, 1, :ROWS].reshape(HALF, D)
    tags = both[:, :, ROWS : ROWS + 3, :ROWS].astype(jnp.int32)
    tags = tags.transpose(2, 1, 0, 3).reshape(3, 2, HALF)
    first = tags[0] * BLOCK
    last = tags[1] * 64 + tags[2]
    lo = (first - half * EVENTS)[:, :, None]
    hi = (last - half * EVENTS)[:, :, None]
    count = (last - first)[0].astype(jnp.float32)

    kv = jnp.stack([hist_key[0], hist_value[0]]).reshape(2, 256, HEADS, HEAD)
    kv = lax.all_to_all(kv.transpose(2, 0, 1, 3), LOCAL, 0, 0, tiled=True)
    keys = kv[:, 0].reshape(EVENTS, HEAD)
    values = kv[:, 1].reshape(EVENTS, HEAD)

    q_other = jnp.dot(normed_other, cols[:, 256:384], preferred_element_type=jnp.float32)
    q_other = silu(q_other).astype(jnp.bfloat16)
    away = attend(q_other, keys, values, lo[1], hi[1], jnp.bfloat16)
    home = lax.ppermute(away, "zh", [(0, 1), (1, 0)])

    proj = jnp.dot(normed_own, cols[:, :512], preferred_element_type=jnp.float32)
    proj = silu(proj).astype(jnp.bfloat16)
    query = proj[:, 256:384]
    own = attend(query, keys, values, lo[0], hi[0], jnp.float32)

    gate = proj[:, :128].astype(jnp.float32)
    val = proj[:, 128:256].astype(jnp.float32)
    key_self = proj[:, 384:512].astype(jnp.float32)
    score = jnp.sum(query.astype(jnp.float32) * key_self, axis=-1, keepdims=True)
    self_term = silu(score * SCALE) * val
    attended = (own + home.astype(jnp.float32) + self_term) / (count[:, None] + 1.0)
    mixed = (layer_norm(attended) * gate).astype(jnp.bfloat16)

    mixed = lax.all_to_all(mixed.reshape(8, ROWS, HEAD), LOCAL, 0, 0, tiled=True)
    mixed = mixed.reshape(8, ROWS, 4, 32).transpose(1, 2, 0, 3).reshape(ROWS, D)
    w_out_all = w_out_all.transpose(1, 0, 2).reshape(D, D)
    projected = jnp.dot(mixed, w_out_all, preferred_element_type=jnp.float32)
    return (x.astype(jnp.float32) + projected).astype(jnp.bfloat16)[None]


def solution(mesh):
    parts = Mesh(mesh.devices.reshape(2, 4, 2, 8, 4), ("zh", "x", "c", "zl", "y"))
    return jax.shard_map(
        body,
        mesh=parts,
        in_specs=(
            P(USER, HIST, None),
            P(USER, HIST, None),
            P(USER, HIST, None),
            P(USER, None),
            P(USER, HIST),
            P(USER, HIST),
            P(USER, None),
            P(USER, None),
        ),
        out_specs=P(USER, HIST, None),
        check_vma=False,
    )
```

```python
import jax
import jax.numpy as jnp
from jax import lax
from jax.experimental import pallas as pl
from jax.experimental.pallas import tpu as pltpu
from jax.sharding import Mesh, PartitionSpec as P

D = 1024
HEADS = 8
HEAD = 128
BLOCK = 128
ROWS = 64
WIDE = D + 128
HALF = 512
EVENTS = 2048
USER = ("zl", "y")
LOCAL = ("x", "c")
HIST = ("zh", "x", "c")
SCALE = HEAD ** (-0.5)
VMEM = pl.BlockSpec(memory_space=pltpu.VMEM)
ANY = pl.BlockSpec(memory_space=pl.ANY)
SMEM = pl.BlockSpec(memory_space=pltpu.SMEM)
PARAMS = pltpu.CompilerParams(vmem_limit_bytes=40 << 20)
F32 = jnp.float32
BF16 = jnp.bfloat16


def silu(v):
    h = v * 0.5
    return h + h * jnp.tanh(h)


def layer_norm(values):
    mean = jnp.mean(values, axis=-1, keepdims=True)
    centred = values - mean
    var = jnp.mean(centred * centred, axis=-1, keepdims=True)
    return centred * lax.rsqrt(var + 1e-05)


def swap(value, axis):
    return lax.ppermute(value, axis, [(0, 1), (1, 0)])


def along_x(value, steps):
    return lax.ppermute(value, "x", [(i, (i + steps) % 4) for i in range(4)])


def prepare_kernel(owner_ref, x_ref, user_ref, cutoff_ref, out_ref):
    out_ref[:, :D] = layer_norm(x_ref[...].astype(F32)).astype(BF16)
    square = (ROWS, ROWS)
    diagonal = lax.broadcasted_iota(jnp.int32, square, 0) == lax.broadcasted_iota(jnp.int32, square, 1)
    user = user_ref[...]
    before = jnp.zeros(user.shape, jnp.int32)
    for b in range(32):
        before = before + (owner_ref[0, b] < user).astype(jnp.int32)

    def column(row):
        spread_out = jnp.where(diagonal, jnp.broadcast_to(row.astype(F32), square), 0.0)
        return jnp.sum(spread_out, axis=1, keepdims=True)

    cutoff = cutoff_ref[...]
    lane = lax.broadcasted_iota(jnp.int32, (ROWS, 128), 1)
    tags = jnp.where(lane == 0, column(before), 0.0)
    tags = jnp.where(lane == 1, column(cutoff >> 6), tags)
    tags = jnp.where(lane == 2, column(cutoff & 63), tags)
    out_ref[:, D:] = tags.astype(BF16)


def prepare(owner, x, user, cutoff):
    return pl.pallas_call(
        prepare_kernel,
        out_shape=jax.ShapeDtypeStruct((ROWS, WIDE), BF16),
        in_specs=[SMEM, VMEM, VMEM, VMEM],
        out_specs=VMEM,
        compiler_params=PARAMS,
    )(owner, x, user, cutoff)


def columns_kernel(place_ref, in_ref, out_w_ref, out_ref):
    head = place_ref[0] * 2 + place_ref[1]
    for part in range(5):
        if part < 4:
            at = pl.ds(pl.multiple_of(head * HEAD + part * D, HEAD), HEAD)
            block = in_ref[:, at]
        else:
            block = out_w_ref[:, pl.ds(pl.multiple_of(head * HEAD, HEAD), HEAD)]
        for copy in range(8):
            out_ref[copy, :, part * HEAD : part * HEAD + HEAD] = block


def columns(*args):
    return pl.pallas_call(
        columns_kernel,
        out_shape=jax.ShapeDtypeStruct((8, 32, 640), BF16),
        in_specs=[SMEM, VMEM, VMEM],
        out_specs=VMEM,
        compiler_params=PARAMS,
    )(*args)


def pairs_kernel(place_ref, k_ref, v_ref, *out_refs):
    for s in range(4):
        at = pl.ds(pl.multiple_of(((place_ref[0] + s) & 3) * 256, 256), 256)
        out_refs[s][0] = k_ref[:, at]
        out_refs[s][1] = v_ref[:, at]


def pairs(*args):
    return pl.pallas_call(
        pairs_kernel,
        out_shape=[jax.ShapeDtypeStruct((2, 256, 256), BF16)] * 4,
        in_specs=[SMEM, VMEM, VMEM],
        out_specs=[VMEM] * 4,
        compiler_params=PARAMS,
    )(*args)


def give_kernel(place_ref, kv0, kv1, kv2, kv3, out_ref):
    at = pl.ds(pl.multiple_of((1 - place_ref[1]) * HEAD, HEAD), HEAD)
    for s, ref in enumerate((kv0, kv1, kv2, kv3)):
        for i in range(2):
            out_ref[s, i] = ref[i, :, at]


def give(*args):
    return pl.pallas_call(
        give_kernel,
        out_shape=jax.ShapeDtypeStruct((4, 2, 256, HEAD), BF16),
        in_specs=[SMEM] + [VMEM] * 4,
        out_specs=VMEM,
        compiler_params=PARAMS,
    )(*args)


def repeat_kernel(cols_ref, *refs):
    out_ref = refs[-1]
    for y in range(4):
        out_ref[y] = cols_ref[...].reshape(256, 640)


def repeat(cols, *after):
    return pl.pallas_call(
        repeat_kernel,
        out_shape=jax.ShapeDtypeStruct((4, 256, 640), BF16),
        in_specs=[VMEM] + [ANY] * len(after),
        out_specs=VMEM,
        compiler_params=PARAMS,
    )(cols, *after)


def out_part_kernel(cols_ref, after_ref, out_ref):
    out_ref[...] = cols_ref[:, :, 512:]


def out_part(*args):
    return pl.pallas_call(
        out_part_kernel,
        out_shape=jax.ShapeDtypeStruct((4, 256, HEAD), BF16),
        in_specs=[VMEM, ANY],
        out_specs=VMEM,
        compiler_params=PARAMS,
    )(*args)


def join_kernel(mine_ref, other_ref, after_ref, out_ref):
    out_ref[0] = mine_ref[...]
    out_ref[1] = other_ref[...]


def join(*args):
    return pl.pallas_call(
        join_kernel,
        out_shape=jax.ShapeDtypeStruct((2, ROWS, WIDE), BF16),
        in_specs=[VMEM, VMEM, ANY],
        out_specs=VMEM,
        compiler_params=PARAMS,
    )(*args)


def load_events(place_ref, kv_refs, peer_ref, k_all, v_all):
    lanes = pl.ds(pl.multiple_of(place_ref[1] * HEAD, HEAD), HEAD)
    for s in range(4):
        k_all[pl.ds(s * 512, 256), :] = kv_refs[s][0, :, lanes]
        v_all[pl.ds(s * 512, 256), :] = kv_refs[s][1, :, lanes]
        k_all[pl.ds(s * 512 + 256, 256), :] = peer_ref[s, 0]
        v_all[pl.ds(s * 512 + 256, 256), :] = peer_ref[s, 1]


def load_weight(w_ref, w_all, first, count):
    for y in range(4):
        for z in range(8):
            w_all[pl.ds(z * 128 + y * 32, 32), :] = w_ref[y, pl.ds(z * 32, 32), pl.ds(first, count)]


def load_rows(which, own_ref, peer_ref, rows):
    for core, ref in enumerate((own_ref, peer_ref)):
        for s in range(4):
            rows[pl.ds(core * 256 + s * ROWS, ROWS), :] = ref[s, which]


def visible(rows, half):
    tags = rows[:, D:].astype(F32)
    first = tags[:, 0:1] * BLOCK
    last = tags[:, 1:2] * 64.0 + tags[:, 2:3]
    return first, last


def attend_rows(place_ref, q_ref, lo_ref, hi_ref, k_all, v_all, store):
    tile, chunk = 128, 512
    x, core, half = place_ref[0], place_ref[1], place_ref[2]

    def rows(i, carry):
        at = pl.ds(pl.multiple_of(i * tile, tile), tile)
        q = q_ref[at, :]
        lo = jnp.broadcast_to(lo_ref[at, :], (tile, 256))
        hi = jnp.broadcast_to(hi_ref[at, :], (tile, 256))
        total = jnp.zeros((tile, HEAD), F32)
        for s in range(4):
            base = half * EVENTS + ((x - s + 4) & 3) * 512
            span = pl.ds(s * chunk, chunk)
            score = lax.dot_general(
                q, k_all[span, :], (((1,), (1,)), ((), ())), preferred_element_type=F32
            )
            parts = []
            for rel in range(2):
                h = score[:, rel * 256 : rel * 256 + 256] * (0.5 * SCALE)
                w = h + h * jnp.tanh(h)
                event = lax.broadcasted_iota(jnp.int32, (tile, 256), 1) + (base + (core ^ rel) * 256)
                seen = (event >= lo) & (event < hi)
                parts.append(jnp.where(seen, w, 0.0).astype(BF16))
            w = jnp.concatenate(parts, axis=1)
            total = total + jnp.dot(w, v_all[span, :], preferred_element_type=F32)
        store(at, total)
        return carry

    lax.fori_loop(0, HALF // tile, rows, 0)


def other_kernel(
    place_ref, own_ref, peer_ref, w_ref, kv0, kv1, kv2, kv3, kv_peer, out_ref,
    rows, w_all, k_all, v_all, q_all, lo_all, hi_all,
):
    load_rows(1, own_ref, peer_ref, rows)
    load_weight(w_ref, w_all, 256, HEAD)
    load_events(place_ref, (kv0, kv1, kv2, kv3), kv_peer, k_all, v_all)
    first, last = visible(rows, 0)
    lo_all[...] = first.astype(jnp.int32)
    hi_all[...] = last.astype(jnp.int32)
    query = jnp.dot(rows[:, :D], w_all[...], preferred_element_type=F32)
    q_all[...] = silu(query).astype(BF16)

    def store(at, total):
        out_ref[at, :] = total.astype(BF16)

    attend_rows(place_ref, q_all, lo_all, hi_all, k_all, v_all, store)


def own_kernel(
    place_ref, own_ref, peer_ref, w_ref, kv0, kv1, kv2, kv3, kv_peer, sum_ref, gate_ref, den_ref,
    rows, w_all, k_all, v_all, q_all, lo_all, hi_all, self_all,
):
    load_rows(0, own_ref, peer_ref, rows)
    load_weight(w_ref, w_all, 0, 512)
    load_events(place_ref, (kv0, kv1, kv2, kv3), kv_peer, k_all, v_all)
    first, last = visible(rows, 0)
    lo_all[...] = first.astype(jnp.int32)
    hi_all[...] = last.astype(jnp.int32)
    den_ref[...] = jnp.broadcast_to(last - first + 1.0, (HALF, HEAD))
    for i in range(2):
        at = pl.ds(i * 256, 256)
        proj = jnp.dot(rows[at, :D], w_all[...], preferred_element_type=F32)
        proj = silu(proj).astype(BF16)
        gate_ref[at, :] = proj[:, 0:128]
        q_all[at, :] = proj[:, 256:384]
        query = proj[:, 256:384].astype(F32)
        score = jnp.sum(query * proj[:, 384:512].astype(F32), axis=-1, keepdims=True)
        self_all[at, :] = silu(score * SCALE) * proj[:, 128:256].astype(F32)

    def store(at, total):
        sum_ref[at, :] = total + self_all[at, :]

    attend_rows(place_ref, q_all, lo_all, hi_all, k_all, v_all, store)


def scratch(columns):
    return [
        pltpu.VMEM((HALF, WIDE), BF16),
        pltpu.VMEM((D, columns), BF16),
        pltpu.VMEM((EVENTS, HEAD), BF16),
        pltpu.VMEM((EVENTS, HEAD), BF16),
        pltpu.VMEM((HALF, HEAD), BF16),
        pltpu.VMEM((HALF, 1), jnp.int32),
        pltpu.VMEM((HALF, 1), jnp.int32),
    ]


def attend_other(*args):
    return pl.pallas_call(
        other_kernel,
        out_shape=jax.ShapeDtypeStruct((HALF, HEAD), BF16),
        in_specs=[SMEM] + [VMEM] * 8,
        out_specs=VMEM,
        scratch_shapes=scratch(HEAD),
        cost_estimate=pl.CostEstimate(
            flops=4 * HALF * EVENTS * HEAD, bytes_accessed=4 << 20, transcendentals=HALF * EVENTS
        ),
        compiler_params=PARAMS,
    )(*args)


def attend_own(*args):
    shape = (HALF, HEAD)
    return pl.pallas_call(
        own_kernel,
        out_shape=[
            jax.ShapeDtypeStruct(shape, F32),
            jax.ShapeDtypeStruct(shape, BF16),
            jax.ShapeDtypeStruct(shape, F32),
        ],
        in_specs=[SMEM] + [VMEM] * 8,
        out_specs=[VMEM] * 3,
        scratch_shapes=scratch(512) + [pltpu.VMEM(shape, F32)],
        cost_estimate=pl.CostEstimate(
            flops=6 * HALF * EVENTS * HEAD, bytes_accessed=4 << 20, transcendentals=HALF * EVENTS
        ),
        compiler_params=PARAMS,
    )(*args)


def mix_kernel(place_ref, sum_ref, home_ref, den_ref, gate_ref, out_ref):
    x, core = place_ref[0], place_ref[1]
    for rel in range(2):
        for s in range(4):
            at = pl.ds(rel * 256 + s * ROWS, ROWS)
            attended = (sum_ref[at, :] + home_ref[at, :].astype(F32)) / den_ref[at, :]
            mixed = layer_norm(attended) * gate_ref[at, :].astype(F32)
            out_ref[((x - s + 4) & 3) * 2 + (core ^ rel)] = mixed.astype(BF16)


def mix(*args):
    return pl.pallas_call(
        mix_kernel,
        out_shape=jax.ShapeDtypeStruct((HEADS, ROWS, HEAD), BF16),
        in_specs=[SMEM] + [VMEM] * 4,
        out_specs=VMEM,
        compiler_params=PARAMS,
    )(*args)


def finish_kernel(x_ref, mixed_ref, w_ref, out_ref, mixed):
    for y in range(4):
        for h in range(HEADS):
            mixed[y, :, h * 32 : h * 32 + 32] = mixed_ref[h, :, y * 32 : y * 32 + 32]
    for part in range(8):
        at = pl.ds(part * HEAD, HEAD)
        total = x_ref[:, at].astype(F32)
        for y in range(4):
            total = total + jnp.dot(mixed[y], w_ref[part, y], preferred_element_type=F32)
        out_ref[:, at] = total.astype(BF16)


def finish(*args):
    return pl.pallas_call(
        finish_kernel,
        out_shape=jax.ShapeDtypeStruct((ROWS, D), BF16),
        in_specs=[VMEM] * 3,
        out_specs=VMEM,
        scratch_shapes=[pltpu.VMEM((4, ROWS, 256), BF16)],
        compiler_params=PARAMS,
    )(*args)


def body(cand_embed, hist_key, hist_value, block_owner, cand_user, cand_cutoff, w_in, w_out):
    x = cand_embed[0]
    place = [lax.axis_index("x"), lax.axis_index("c"), lax.axis_index("zh")]
    place = jnp.stack(place).astype(jnp.int32)

    mine = prepare(block_owner, x, cand_user, cand_cutoff)
    other = swap(mine, "zh")

    cols = lax.all_to_all(columns(place, w_in, w_out), "zl", 0, 0, tiled=True)

    kv = pairs(place, hist_key[0], hist_value[0])
    kv = [along_x(pair, s) if s else pair for s, pair in enumerate(kv)]
    kv_peer = swap(give(place, *kv), "c")

    cols = repeat(cols, other, *kv[1:])
    both = join(mine, other, cols)
    cols = lax.all_to_all(cols, "y", 0, 0, tiled=True)
    own_core = jnp.stack([along_x(both, s) if s else both for s in range(4)])
    peer_core = swap(own_core, "c")

    args = (place, own_core, peer_core, cols, *kv, kv_peer)
    away = attend_other(*args)
    home = swap(away, "zh")
    sums, gate, den = attend_own(*args)

    w_all = lax.all_gather(out_part(cols, own_core), LOCAL, axis=0)

    mixed = mix(place, sums, home, den, gate)
    mixed = lax.all_to_all(mixed, LOCAL, 0, 0, tiled=True)
    return finish(x, mixed, w_all)[None]


def solution(mesh):
    parts = Mesh(mesh.devices.reshape(2, 4, 2, 8, 4), ("zh", "x", "c", "zl", "y"))
    return jax.shard_map(
        body,
        mesh=parts,
        in_specs=(
            P(USER, HIST, None),
            P(USER, HIST, None),
            P(USER, HIST, None),
            P(USER, None),
            P(USER, HIST),
            P(USER, HIST),
            P(USER, None),
            P(USER, None),
        ),
        out_specs=P(USER, HIST, None),
        check_vma=False,
    )
```

```python
import jax
import jax.numpy as jnp
from jax import lax
from jax.experimental import pallas as pl
from jax.experimental.pallas import tpu as pltpu
from jax.sharding import Mesh, PartitionSpec as P

D = 1024
HEADS = 8
HEAD = 128
BLOCK = 128
ROWS = 64
WIDE = D + 128
KV_ROWS = 1024
MY_ROWS = 576
HALF = 512
EVENTS = 2048
USER = ("zl", "y")
LOCAL = ("x", "c")
HIST = ("zh", "x", "c")
SCALE = HEAD ** (-0.5)
VMEM = pl.BlockSpec(memory_space=pltpu.VMEM)
ANY = pl.BlockSpec(memory_space=pl.ANY)
SMEM = pl.BlockSpec(memory_space=pltpu.SMEM)
PARAMS = pltpu.CompilerParams(vmem_limit_bytes=16 << 20)
WHOLE = pltpu.CompilerParams(vmem_limit_bytes=60 << 20)

def cost(megabytes):
    return pl.CostEstimate(flops=megabytes << 28, bytes_accessed=megabytes << 20, transcendentals=megabytes << 18)


C_PACKETS, C_COLS, C_OTHER, C_AWAY, C_OWN, C_MIX = 1, 2000, 1, 4, 4, 2000
F32 = jnp.float32
BF16 = jnp.bfloat16


def silu(v):
    h = v * 0.5
    return h + h * jnp.tanh(h)


def layer_norm(values):
    mean = jnp.mean(values, axis=-1, keepdims=True)
    centred = values - mean
    var = jnp.mean(centred * centred, axis=-1, keepdims=True)
    return centred * lax.rsqrt(var + 1e-05)


def swap(value, axis):
    return lax.ppermute(value, axis, [(0, 1), (1, 0)])


def along(value, axis, steps):
    return lax.ppermute(value, axis, [(i, (i + steps) % 4) for i in range(4)])


def prepare_kernel(owner_ref, x_ref, user_ref, cutoff_ref, after_ref, out_ref):
    out_ref[:, :D] = layer_norm(x_ref[...].astype(F32)).astype(BF16)
    square = (ROWS, ROWS)
    diagonal = lax.broadcasted_iota(jnp.int32, square, 0) == lax.broadcasted_iota(jnp.int32, square, 1)
    user = user_ref[...]
    before = jnp.zeros(user.shape, jnp.int32)
    for b in range(32):
        before = before + (owner_ref[0, b] < user).astype(jnp.int32)

    def column(row):
        spread_out = jnp.where(diagonal, jnp.broadcast_to(row.astype(F32), square), 0.0)
        return jnp.sum(spread_out, axis=1, keepdims=True)

    cutoff = cutoff_ref[...]
    lane = lax.broadcasted_iota(jnp.int32, (ROWS, 128), 1)
    tags = jnp.where(lane == 0, column(before), 0.0)
    tags = jnp.where(lane == 1, column(cutoff >> 6), tags)
    tags = jnp.where(lane == 2, column(cutoff & 63), tags)
    out_ref[:, D:] = tags.astype(BF16)


def prepare(*args):
    return pl.pallas_call(
        prepare_kernel,
        name="prepare",
        out_shape=jax.ShapeDtypeStruct((ROWS, WIDE), BF16),
        in_specs=[SMEM, VMEM, VMEM, VMEM, ANY],
        out_specs=VMEM,
        compiler_params=WHOLE,
    )(*args)


def columns_kernel(place_ref, in_ref, out_w_ref, out_ref, block, sems):
    first = (place_ref[0] * 2 + place_ref[1]) * HEAD
    copies = []
    for part in range(5):
        ref, start = (in_ref, first + part * D) if part < 4 else (out_w_ref, first)
        at = pl.ds(pl.multiple_of(start, HEAD), HEAD)
        to = block.at[:, pl.ds(part * HEAD, HEAD)]
        copies.append(pltpu.make_async_copy(ref.at[:, at], to, sems.at[part]))
        copies[part].start()
    for copy in copies:
        copy.wait()
    for z in range(8):
        out_ref[z] = block[...]


def columns(*args):
    return pl.pallas_call(
        columns_kernel,
        name="columns",
        out_shape=jax.ShapeDtypeStruct((8, 32, 640), BF16),
        in_specs=[SMEM, ANY, ANY],
        out_specs=VMEM,
        scratch_shapes=[pltpu.VMEM((32, 640), BF16), pltpu.SemaphoreType.DMA((5,))],
        compiler_params=WHOLE,
    )(*args)


def packets_kernel(place_ref, k_ref, v_ref, mine_ref, *out_refs):
    for s in range(4):
        for core in range(2):
            start = ((place_ref[0] + s) & 3) * 256 + core * HEAD
            at = pl.ds(pl.multiple_of(start, HEAD), HEAD)
            out_refs[s][core * 256 : core * 256 + 256, :] = k_ref[:, at]
            out_refs[s][512 + core * 256 : 768 + core * 256, :] = v_ref[:, at]
        for part in range(9):
            to = KV_ROWS + part * ROWS
            out_refs[s][to : to + ROWS, :] = mine_ref[:, part * HEAD : part * HEAD + HEAD]


def packets(*args):
    return pl.pallas_call(
        packets_kernel,
        name="packets",
        out_shape=[jax.ShapeDtypeStruct((KV_ROWS + MY_ROWS, HEAD), BF16)] * 4,
        in_specs=[SMEM, VMEM, VMEM, VMEM],
        out_specs=[VMEM] * 4,
        cost_estimate=cost(C_PACKETS),
        compiler_params=PARAMS,
    )(*args)


def give_kernel(place_ref, p0, p1, p2, p3, *refs):
    out_ref = refs[-1]
    other = 1 - place_ref[1]
    for s, ref in enumerate((p0, p1, p2, p3)):
        for i in range(2):
            at = pl.ds(pl.multiple_of(i * 512 + other * 256, 256), 256)
            out_ref[s, i * 256 : i * 256 + 256, :] = ref[at, :]
        out_ref[s, 512:, :] = ref[KV_ROWS:, :]


def give(*args):
    return pl.pallas_call(
        give_kernel,
        name="give",
        out_shape=jax.ShapeDtypeStruct((4, 512 + MY_ROWS, HEAD), BF16),
        in_specs=[SMEM] + [VMEM] * 4 + [ANY] * 6,
        out_specs=VMEM,
        compiler_params=PARAMS,
    )(*args)


def out_part_kernel(w0, w1, w2, w3, out_ref):
    for s, ref in enumerate((w0, w1, w2, w3)):
        out_ref[s] = ref[:, 512:]


def out_part(*args):
    return pl.pallas_call(
        out_part_kernel,
        name="out_part",
        out_shape=jax.ShapeDtypeStruct((4, 256, HEAD), BF16),
        in_specs=[VMEM] * 4,
        out_specs=VMEM,
        compiler_params=PARAMS,
    )(*args)


def hold_kernel(*refs):
    refs[-1][...] = refs[0][...]


def hold(value, estimate, *after):
    return pl.pallas_call(
        hold_kernel,
        name="hold",
        out_shape=jax.ShapeDtypeStruct(value.shape, value.dtype),
        in_specs=[VMEM] + [ANY] * len(after),
        out_specs=VMEM,
        cost_estimate=cost(estimate),
        compiler_params=PARAMS,
    )(value, *after)


def stack_kernel(*refs):
    for s in range(4):
        refs[-1][s] = refs[s][...]


def stack(first, *rest):
    return pl.pallas_call(
        stack_kernel,
        name="stack",
        out_shape=jax.ShapeDtypeStruct((4,) + first.shape, BF16),
        in_specs=[VMEM] * 4 + [ANY] * (len(rest) - 3),
        out_specs=VMEM,
        compiler_params=PARAMS,
    )(first, *rest)


def load_events(place_ref, packet_refs, peer_ref, k_all, v_all):
    core = place_ref[1]
    for s, ref in enumerate(packet_refs):
        for i, to in enumerate((k_all, v_all)):
            at = pl.ds(pl.multiple_of(i * 512 + core * 256, 256), 256)
            to[pl.ds(s * 512, 256), :] = ref[at, :]
            to[pl.ds(s * 512 + 256, 256), :] = peer_ref[s, i * 256 : i * 256 + 256, :]


def load_weight(place_ref, w_refs, w_all, first, count):
    for s, ref in enumerate(w_refs):
        y = (place_ref[3] - s + 4) & 3
        for z in range(8):
            at = pl.ds(pl.multiple_of(z * 128 + y * 32, 32), 32)
            w_all[at, :] = ref[pl.ds(z * 32, 32), pl.ds(first, count)]


def load_own_rows(packet_refs, peer_ref, rows):
    for s, ref in enumerate(packet_refs):
        for part in range(9):
            at = pl.ds(part * HEAD, HEAD)
            to, start = s * ROWS, KV_ROWS + part * ROWS
            rows[to : to + ROWS, at] = ref[start : start + ROWS, :]
            start = 512 + part * ROWS
            rows[256 + to : 256 + to + ROWS, at] = peer_ref[s, start : start + ROWS, :]


def load_other_rows(own_ref, peer_ref, rows):
    for core, ref in enumerate((own_ref, peer_ref)):
        for s in range(4):
            rows[pl.ds(core * 256 + s * ROWS, ROWS), :] = ref[s]


def visible(rows, half):
    tags = rows[:, D:].astype(F32)
    first = tags[:, 0:1] * BLOCK
    last = tags[:, 1:2] * 64.0 + tags[:, 2:3]
    return first, last


def attend_rows(place_ref, q_ref, lo_ref, hi_ref, k_all, v_all, store):
    tile, chunk = 128, 512
    x, core, half = place_ref[0], place_ref[1], place_ref[2]

    def rows(i, carry):
        at = pl.ds(pl.multiple_of(i * tile, tile), tile)
        q = q_ref[at, :]
        lo = jnp.broadcast_to(lo_ref[at, :], (tile, 256))
        hi = jnp.broadcast_to(hi_ref[at, :], (tile, 256))
        total = jnp.zeros((tile, HEAD), F32)
        for s in range(4):
            base = half * EVENTS + ((x - s + 4) & 3) * 512
            span = pl.ds(s * chunk, chunk)
            score = lax.dot_general(
                q, k_all[span, :], (((1,), (1,)), ((), ())), preferred_element_type=F32
            )
            parts = []
            for rel in range(2):
                h = score[:, rel * 256 : rel * 256 + 256] * (0.5 * SCALE)
                w = h + h * jnp.tanh(h)
                event = lax.broadcasted_iota(jnp.int32, (tile, 256), 1) + (base + (core ^ rel) * 256)
                seen = (event >= lo) & (event < hi)
                parts.append(jnp.where(seen, w, 0.0).astype(BF16))
            w = jnp.concatenate(parts, axis=1)
            total = total + jnp.dot(w, v_all[span, :], preferred_element_type=F32)
        store(at, total)
        return carry

    lax.fori_loop(0, HALF // tile, rows, 0)


def other_kernel(
    place_ref, own_ref, peer_ref, w0, w1, w2, w3, p0, p1, p2, p3, kv_peer, out_ref,
    rows, w_all, k_all, v_all, q_all, lo_all, hi_all,
):
    load_other_rows(own_ref, peer_ref, rows)
    load_weight(place_ref, (w0, w1, w2, w3), w_all, 256, HEAD)
    load_events(place_ref, (p0, p1, p2, p3), kv_peer, k_all, v_all)
    first, last = visible(rows, 0)
    lo_all[...] = first.astype(jnp.int32)
    hi_all[...] = last.astype(jnp.int32)
    query = jnp.dot(rows[:, :D], w_all[...], preferred_element_type=F32)
    q_all[...] = silu(query).astype(BF16)

    def store(at, total):
        out_ref[at, :] = total.astype(BF16)

    attend_rows(place_ref, q_all, lo_all, hi_all, k_all, v_all, store)


def own_kernel(
    place_ref, w0, w1, w2, w3, p0, p1, p2, p3, kv_peer, after_ref, sum_ref, gate_ref, den_ref,
    rows, w_all, k_all, v_all, q_all, lo_all, hi_all, self_all,
):
    load_own_rows((p0, p1, p2, p3), kv_peer, rows)
    load_weight(place_ref, (w0, w1, w2, w3), w_all, 0, 512)
    load_events(place_ref, (p0, p1, p2, p3), kv_peer, k_all, v_all)
    first, last = visible(rows, 0)
    lo_all[...] = first.astype(jnp.int32)
    hi_all[...] = last.astype(jnp.int32)
    den_ref[...] = jnp.broadcast_to(last - first + 1.0, (HALF, HEAD))
    for i in range(2):
        at = pl.ds(i * 256, 256)
        proj = jnp.dot(rows[at, :D], w_all[...], preferred_element_type=F32)
        proj = silu(proj).astype(BF16)
        gate_ref[at, :] = proj[:, 0:128]
        q_all[at, :] = proj[:, 256:384]
        query = proj[:, 256:384].astype(F32)
        score = jnp.sum(query * proj[:, 384:512].astype(F32), axis=-1, keepdims=True)
        self_all[at, :] = silu(score * SCALE) * proj[:, 128:256].astype(F32)

    def store(at, total):
        sum_ref[at, :] = total + self_all[at, :]

    attend_rows(place_ref, q_all, lo_all, hi_all, k_all, v_all, store)


def scratch(columns):
    return [
        pltpu.VMEM((HALF, WIDE), BF16),
        pltpu.VMEM((D, columns), BF16),
        pltpu.VMEM((EVENTS, HEAD), BF16),
        pltpu.VMEM((EVENTS, HEAD), BF16),
        pltpu.VMEM((HALF, HEAD), BF16),
        pltpu.VMEM((HALF, 1), jnp.int32),
        pltpu.VMEM((HALF, 1), jnp.int32),
    ]


def attend_other(*args):
    return pl.pallas_call(
        other_kernel,
        name="other",
        out_shape=jax.ShapeDtypeStruct((HALF, HEAD), BF16),
        in_specs=[SMEM] + [VMEM] * 11,
        out_specs=VMEM,
        scratch_shapes=scratch(HEAD),
        cost_estimate=cost(C_AWAY),
        compiler_params=PARAMS,
    )(*args)


def attend_own(*args):
    shape = (HALF, HEAD)
    return pl.pallas_call(
        own_kernel,
        name="own",
        out_shape=[
            jax.ShapeDtypeStruct(shape, F32),
            jax.ShapeDtypeStruct(shape, BF16),
            jax.ShapeDtypeStruct(shape, F32),
        ],
        in_specs=[SMEM] + [VMEM] * 9 + [ANY],
        out_specs=[VMEM] * 3,
        scratch_shapes=scratch(512) + [pltpu.VMEM(shape, F32)],
        cost_estimate=cost(C_OWN),
        compiler_params=PARAMS,
    )(*args)


def mix_kernel(place_ref, sum_ref, home_ref, den_ref, gate_ref, out_ref):
    x, core = place_ref[0], place_ref[1]
    for rel in range(2):
        for s in range(4):
            at = pl.ds(rel * 256 + s * ROWS, ROWS)
            attended = (sum_ref[at, :] + home_ref[at, :].astype(F32)) / den_ref[at, :]
            mixed = layer_norm(attended) * gate_ref[at, :].astype(F32)
            out_ref[((x - s + 4) & 3) * 2 + (core ^ rel)] = mixed.astype(BF16)


def mix(*args):
    return pl.pallas_call(
        mix_kernel,
        name="mix",
        out_shape=jax.ShapeDtypeStruct((HEADS, ROWS, HEAD), BF16),
        in_specs=[SMEM] + [VMEM] * 4,
        out_specs=VMEM,
        cost_estimate=cost(C_MIX),
        compiler_params=PARAMS,
    )(*args)


def finish_kernel(place_ref, x_ref, mixed_ref, own_ref, peer_ref, out_ref, mixed):
    along, core, line = place_ref[0], place_ref[1], place_ref[3]
    for y in range(4):
        for h in range(HEADS):
            mixed[y, :, h * 32 : h * 32 + 32] = mixed_ref[h, :, y * 32 : y * 32 + 32]
    for s in range(4):
        for rel, ref in enumerate((own_ref, peer_ref)):
            at = ((along - s + 4) & 3) * 2 + (core ^ rel)
            at = pl.ds(pl.multiple_of(at * HEAD, HEAD), HEAD)
            total = x_ref[:, at].astype(F32)
            for step in range(4):
                left = mixed[(line - step + 4) & 3]
                total = total + jnp.dot(left, ref[s, step], preferred_element_type=F32)
            out_ref[:, at] = total.astype(BF16)


def finish(*args):
    return pl.pallas_call(
        finish_kernel,
        name="finish",
        out_shape=jax.ShapeDtypeStruct((ROWS, D), BF16),
        in_specs=[SMEM] + [VMEM] * 4,
        out_specs=VMEM,
        scratch_shapes=[pltpu.VMEM((4, ROWS, 256), BF16)],
        compiler_params=PARAMS,
    )(*args)


def body(cand_embed, hist_key, hist_value, block_owner, cand_user, cand_cutoff, w_in, w_out):
    x = cand_embed[0]
    place = [lax.axis_index("x"), lax.axis_index("c"), lax.axis_index("zh"), lax.axis_index("y")]
    place = jnp.stack(place).astype(jnp.int32)

    cols = columns(place, w_in, w_out)
    mine = prepare(block_owner, x, cand_user, cand_cutoff, cols)
    other = swap(mine, "zh")
    cols = lax.all_to_all(cols, "zl", 0, 0, tiled=True)

    out = packets(place, hist_key[0], hist_value[0], mine)
    packs = [along(pack, "x", s) if s else pack for s, pack in enumerate(out)]
    cols = hold(cols.reshape(256, 640), C_COLS, other)
    other = hold(other, C_OTHER, cols)
    cols = [along(cols, "y", s) if s else cols for s in range(4)]
    others = [along(other, "x", s) if s else other for s in range(4)]
    kv_peer = swap(give(place, *packs, *cols[1:], *others[1:]), "c")
    own_core = stack(*others)
    peer_core = swap(own_core, "c")
    w_part = out_part(*cols)
    w_part = [along(w_part, "x", s) if s else w_part for s in range(4)]

    away = attend_other(place, own_core, peer_core, *cols, *packs, kv_peer)
    home = swap(away, "zh")
    sums, gate, den = attend_own(place, *cols, *packs, kv_peer, away)
    w_own = stack(*w_part, away)
    w_peer = swap(w_own, "c")

    mixed = mix(place, sums, home, den, gate)
    mixed = lax.all_to_all(mixed, LOCAL, 0, 0, tiled=True)
    return finish(place, x, mixed, w_own, w_peer)[None]


def solution(mesh):
    parts = Mesh(mesh.devices.reshape(2, 4, 2, 8, 4), ("zh", "x", "c", "zl", "y"))
    return jax.shard_map(
        body,
        mesh=parts,
        in_specs=(
            P(USER, HIST, None),
            P(USER, HIST, None),
            P(USER, HIST, None),
            P(USER, None),
            P(USER, HIST),
            P(USER, HIST),
            P(USER, None),
            P(USER, None),
        ),
        out_specs=P(USER, HIST, None),
        check_vma=False,
    )
```

```python
import jax
import jax.numpy as jnp
from jax import lax
from jax.experimental import pallas as pl
from jax.experimental.pallas import tpu as pltpu
from jax.sharding import Mesh, PartitionSpec as P

D = 1024
HEADS = 8
HEAD = 128
BLOCK = 128
ROWS = 64
WIDE = D + 128
KV_ROWS = 1024
MY_ROWS = 576
HALF = 512
EVENTS = 2048
USER = ("zl", "y")
LOCAL = ("x", "c")
HIST = ("zh", "x", "c")
SCALE = HEAD ** (-0.5)
VMEM = pl.BlockSpec(memory_space=pltpu.VMEM)
ANY = pl.BlockSpec(memory_space=pl.ANY)
SMEM = pl.BlockSpec(memory_space=pltpu.SMEM)
PARAMS = pltpu.CompilerParams(vmem_limit_bytes=16 << 20)
WHOLE = pltpu.CompilerParams(vmem_limit_bytes=60 << 20)

def cost(megabytes):
    return pl.CostEstimate(flops=megabytes << 28, bytes_accessed=megabytes << 20, transcendentals=megabytes << 18)


C_PARTS, C_PACKETS, C_PROJECT, C_AWAY, C_OWN, C_MIX = 1, 1, 4, 4, 4, 2000
F32 = jnp.float32
BF16 = jnp.bfloat16


def silu(v):
    h = v * 0.5
    return h + h * jnp.tanh(h)


def layer_norm(values):
    mean = jnp.mean(values, axis=-1, keepdims=True)
    centred = values - mean
    var = jnp.mean(centred * centred, axis=-1, keepdims=True)
    return centred * lax.rsqrt(var + 1e-05)


def swap(value, axis):
    return lax.ppermute(value, axis, [(0, 1), (1, 0)])


def along(value, axis, steps):
    return lax.ppermute(value, axis, [(i, (i + steps) % 4) for i in range(4)])


def columns_kernel(in_ref, out_w_ref, out_ref, block, sems):
    first = (lax.axis_index("x") * 2 + lax.axis_index("c")) * HEAD
    copies = []
    for part in range(5):
        ref, start = (in_ref, first + part * D) if part < 4 else (out_w_ref, first)
        at = pl.ds(pl.multiple_of(start, HEAD), HEAD)
        to = block.at[:, pl.ds(part * HEAD, HEAD)]
        copies.append(pltpu.make_async_copy(ref.at[:, at], to, sems.at[part]))
        copies[part].start()
    for copy in copies:
        copy.wait()
    for z in range(8):
        out_ref[z] = block[...]


def columns(*args):
    return pl.pallas_call(
        columns_kernel,
        name="columns",
        out_shape=jax.ShapeDtypeStruct((8, 32, 640), BF16),
        in_specs=[ANY, ANY],
        out_specs=VMEM,
        scratch_shapes=[pltpu.VMEM((32, 640), BF16), pltpu.SemaphoreType.DMA((5,))],
        compiler_params=WHOLE,
    )(*args)


def tags_of(owner_ref, user, cutoff):
    square = (ROWS, ROWS)
    diagonal = lax.broadcasted_iota(jnp.int32, square, 0) == lax.broadcasted_iota(jnp.int32, square, 1)
    before = jnp.zeros(user.shape, jnp.int32)
    for b in range(32):
        before = before + (owner_ref[0, b] < user).astype(jnp.int32)

    def column(row):
        spread_out = jnp.where(diagonal, jnp.broadcast_to(row.astype(F32), square), 0.0)
        return jnp.sum(spread_out, axis=1, keepdims=True)

    lane = lax.broadcasted_iota(jnp.int32, (ROWS, 128), 1)
    tags = jnp.where(lane == 0, column(before), 0.0)
    tags = jnp.where(lane == 1, column(cutoff >> 6), tags)
    return jnp.where(lane == 2, column(cutoff & 63), tags)


def parts_kernel(
    place_ref, owner_ref, x_ref, user_ref, cutoff_ref, k_ref, v_ref, keep_ref, give_ref, rest_ref
):
    along, core = place_ref[0], place_ref[1]
    normed = layer_norm(x_ref[...].astype(F32)).astype(BF16)
    for part in range(8):
        give_ref[part * ROWS : part * ROWS + ROWS, :] = normed[:, part * HEAD : part * HEAD + HEAD]
    tags = tags_of(owner_ref, user_ref[...], cutoff_ref[...]).astype(BF16)
    give_ref[8 * ROWS : MY_ROWS, :] = tags
    keep_ref[2048:, :] = give_ref[0:MY_ROWS, :]
    places = ((give_ref, MY_ROWS), (rest_ref, 0), (rest_ref, 512), (rest_ref, 1024))
    for s in range(4):
        for (to, base), which in (((keep_ref, s * 512), core), (places[s], 1 - core)):
            start = ((along + s) & 3) * 256 + which * HEAD
            at = pl.ds(pl.multiple_of(start, HEAD), HEAD)
            to[base : base + 256, :] = k_ref[:, at]
            to[base + 256 : base + 512, :] = v_ref[:, at]


def parts(*args):
    rows = (2048 + MY_ROWS, MY_ROWS + 512, 1536)
    return pl.pallas_call(
        parts_kernel,
        name="parts",
        out_shape=[jax.ShapeDtypeStruct((n, HEAD), BF16) for n in rows],
        in_specs=[SMEM, SMEM] + [VMEM] * 5,
        out_specs=[VMEM] * 3,
        cost_estimate=cost(C_PARTS),
        compiler_params=PARAMS,
    )(*args)


def packets_kernel(keep_ref, got_ref, rest_ref, *out_refs):
    for s, ref in enumerate(out_refs):
        ref[0:512, :] = keep_ref[s * 512 : s * 512 + 512, :]
        if s == 0:
            ref[512:1024, :] = got_ref[MY_ROWS:, :]
        else:
            ref[512:1024, :] = rest_ref[s * 512 - 512 : s * 512, :]
        ref[KV_ROWS : KV_ROWS + MY_ROWS, :] = keep_ref[2048:, :]
        ref[KV_ROWS + MY_ROWS :, :] = got_ref[0:MY_ROWS, :]


def packets(*args):
    return pl.pallas_call(
        packets_kernel,
        name="packets",
        out_shape=[jax.ShapeDtypeStruct((KV_ROWS + 2 * MY_ROWS, HEAD), BF16)] * 4,
        in_specs=[VMEM] * 3,
        out_specs=[VMEM] * 4,
        cost_estimate=cost(C_PACKETS),
        compiler_params=PARAMS,
    )(*args)


def out_part_kernel(w0, w1, w2, w3, after_ref, out_ref):
    for s, ref in enumerate((w0, w1, w2, w3)):
        out_ref[s] = ref[:, 512:]


def out_part(*args):
    return pl.pallas_call(
        out_part_kernel,
        name="out_part",
        out_shape=jax.ShapeDtypeStruct((4, 256, HEAD), BF16),
        in_specs=[VMEM] * 4 + [ANY],
        out_specs=VMEM,
        compiler_params=PARAMS,
    )(*args)


def stack_kernel(*refs):
    for s in range(4):
        refs[-1][s] = refs[s][...]


def stack(first, *rest):
    return pl.pallas_call(
        stack_kernel,
        name="stack",
        out_shape=jax.ShapeDtypeStruct((4,) + first.shape, BF16),
        in_specs=[VMEM] * 4 + [ANY] * (len(rest) - 3),
        out_specs=VMEM,
        compiler_params=PARAMS,
    )(first, *rest)


def load_weight(place_ref, w_refs, w_all, first, count):
    for s, ref in enumerate(w_refs):
        y = (place_ref[3] - s + 4) & 3
        for z in range(8):
            at = pl.ds(pl.multiple_of(z * 128 + y * 32, 32), 32)
            w_all[at, :] = ref[pl.ds(z * 32, 32), pl.ds(first, count)]


def load_rows(packet_refs, rows):
    for s, ref in enumerate(packet_refs):
        for rel in range(2):
            for part in range(9):
                to, start = rel * 256 + s * ROWS, KV_ROWS + rel * MY_ROWS + part * ROWS
                rows[to : to + ROWS, pl.ds(part * HEAD, HEAD)] = ref[start : start + ROWS, :]


def visible(tags):
    return tags[:, 0:1] * BLOCK, tags[:, 1:2] * 64.0 + tags[:, 2:3]


def project_kernel(
    place_ref, w0, w1, w2, w3, p0, p1, p2, p3,
    query_ref, gate_ref, den_ref, self_ref, rows, w_all,
):
    load_rows((p0, p1, p2, p3), rows)
    load_weight(place_ref, (w0, w1, w2, w3), w_all, 0, 512)
    for i in range(2):
        at = pl.ds(i * 256, 256)
        proj = jnp.dot(rows[at, :D], w_all[...], preferred_element_type=F32)
        proj = silu(proj).astype(BF16)
        gate_ref[at, :] = proj[:, 0:128]
        query_ref[at, :] = proj[:, 256:384]
        query = proj[:, 256:384].astype(F32)
        score = jnp.sum(query * proj[:, 384:512].astype(F32), axis=-1, keepdims=True)
        self_ref[at, :] = silu(score * SCALE) * proj[:, 128:256].astype(F32)
    for i in range(4):
        at = pl.ds(i * 128, 128)
        tags = rows[at, D:].astype(F32)
        first, last = visible(tags)
        den_ref[at, :] = jnp.broadcast_to(last - first + 1.0, (128, HEAD))
        query_ref[HALF + i * 16 : HALF + i * 16 + 16, :] = tags.T[0:16, :].astype(BF16)


def project(*args):
    shape = (HALF, HEAD)
    return pl.pallas_call(
        project_kernel,
        name="project",
        out_shape=[
            jax.ShapeDtypeStruct((HALF + 64, HEAD), BF16),
            jax.ShapeDtypeStruct(shape, BF16),
            jax.ShapeDtypeStruct(shape, F32),
            jax.ShapeDtypeStruct(shape, F32),
        ],
        in_specs=[SMEM] + [VMEM] * 8,
        out_specs=[VMEM] * 4,
        scratch_shapes=[pltpu.VMEM((HALF, WIDE), BF16), pltpu.VMEM((D, 512), BF16)],
        cost_estimate=cost(C_PROJECT),
        compiler_params=PARAMS,
    )(*args)


def attend_kernel(place_ref, q_ref, p0, p1, p2, p3, plus_ref, out_ref):
    x, core, half = place_ref[0], place_ref[1], place_ref[2]
    event = lax.broadcasted_iota(jnp.int32, (256, 256), 1)
    for tile in range(2):
        at = pl.ds(tile * 256, 256)
        lows, counts = [], []
        for i in range(2):
            row = HALF + (tile * 2 + i) * 16
            tags = q_ref[row : row + 16, :].astype(F32)
            tags = jnp.concatenate([tags, jnp.zeros((112, 128), F32)], axis=0).T
            first, last = visible(tags)
            lows.append(first.astype(jnp.int32))
            counts.append((last - first).astype(jnp.uint32))
        low = jnp.broadcast_to(jnp.concatenate(lows, axis=0), (256, 256))
        count = jnp.broadcast_to(jnp.concatenate(counts, axis=0), (256, 256))
        query = q_ref[at, :]
        total = jnp.zeros((256, HEAD), F32)
        for s, ref in enumerate((p0, p1, p2, p3)):
            for rel in range(2):
                base = half * EVENTS + ((x - s + 4) & 3) * 512 + (core ^ rel) * 256
                row = rel * 512
                score = lax.dot_general(
                    query, ref[row : row + 256, :], (((1,), (1,)), ((), ())), preferred_element_type=F32
                )
                h = score * (0.5 * SCALE)
                w = h + h * jnp.tanh(h)
                seen = (event + base - low).astype(jnp.uint32) < count
                w = jnp.where(seen, w, 0.0).astype(BF16)
                total = total + jnp.dot(w, ref[row + 256 : row + 512, :], preferred_element_type=F32)
        if out_ref.dtype == F32:
            total = total + plus_ref[at, :]
        out_ref[at, :] = total.astype(out_ref.dtype)


def attend(name, dtype, *args):
    return pl.pallas_call(
        attend_kernel,
        name=name,
        out_shape=jax.ShapeDtypeStruct((HALF, HEAD), dtype),
        in_specs=[SMEM] + [VMEM] * 6,
        out_specs=VMEM,
        cost_estimate=cost(C_AWAY if name == "other" else C_OWN),
        compiler_params=PARAMS,
    )(*args)


def mix_kernel(place_ref, sum_ref, home_ref, den_ref, gate_ref, out_ref):
    x, core = place_ref[0], place_ref[1]
    for rel in range(2):
        for s in range(4):
            at = pl.ds(rel * 256 + s * ROWS, ROWS)
            attended = (sum_ref[at, :] + home_ref[at, :].astype(F32)) / den_ref[at, :]
            mixed = layer_norm(attended) * gate_ref[at, :].astype(F32)
            out_ref[((x - s + 4) & 3) * 2 + (core ^ rel)] = mixed.astype(BF16)


def mix(*args):
    return pl.pallas_call(
        mix_kernel,
        name="mix",
        out_shape=jax.ShapeDtypeStruct((HEADS, ROWS, HEAD), BF16),
        in_specs=[SMEM] + [VMEM] * 4,
        out_specs=VMEM,
        cost_estimate=cost(C_MIX),
        compiler_params=PARAMS,
    )(*args)


def finish_kernel(place_ref, x_ref, mixed_ref, w0, w1, w2, w3, peer_ref, out_ref, by_line):
    along, core, line = place_ref[0], place_ref[1], place_ref[3]
    for y in range(4):
        for h in range(HEADS):
            by_line[y, :, h * 32 : h * 32 + 32] = mixed_ref[h, :, y * 32 : y * 32 + 32]
    left = jnp.concatenate([by_line[(line - step + 4) & 3] for step in range(4)], axis=1)
    for s, ref in enumerate((w0, w1, w2, w3)):
        for rel in range(2):
            at = ((along - s + 4) & 3) * 2 + (core ^ rel)
            at = pl.ds(pl.multiple_of(at * HEAD, HEAD), HEAD)
            right = (ref[...] if rel == 0 else peer_ref[s]).reshape(D, HEAD)
            projected = jnp.dot(left, right, preferred_element_type=F32)
            out_ref[:, at] = (x_ref[:, at].astype(F32) + projected).astype(BF16)


def finish(*args):
    return pl.pallas_call(
        finish_kernel,
        name="finish",
        out_shape=jax.ShapeDtypeStruct((ROWS, D), BF16),
        in_specs=[SMEM] + [VMEM] * 7,
        out_specs=VMEM,
        scratch_shapes=[pltpu.VMEM((4, ROWS, 256), BF16)],
        compiler_params=PARAMS,
    )(*args)


def body(cand_embed, hist_key, hist_value, block_owner, cand_user, cand_cutoff, w_in, w_out):
    x = cand_embed[0]
    place = [lax.axis_index(a) for a in ("x", "c", "zh", "y")]
    place = jnp.stack(place).astype(jnp.int32)

    cols = columns(w_in, w_out)
    cols = lax.all_to_all(cols, "zl", 0, 0, tiled=True).reshape(256, 640)
    cols = [along(cols, "y", s) if s else cols for s in range(4)]

    keep, *got = parts(place, block_owner, x, cand_user, cand_cutoff, hist_key[0], hist_value[0])
    packs = packets(keep, *[swap(part, "c") for part in got])
    packs = [along(pack, "x", s) if s else pack for s, pack in enumerate(packs)]

    query, gate, den, self_term = project(place, *cols, *packs)
    query_other = swap(query, "zh")

    w_part = out_part(*cols, query)
    w_part = [along(w_part, "x", s) if s else w_part for s in range(4)]

    away = attend("other", BF16, place, query_other, *packs, self_term)
    home = swap(away, "zh")
    sums = attend("own", F32, place, query, *packs, self_term)
    w_own = stack(*w_part, away)
    w_peer = swap(w_own, "c")

    mixed = mix(place, sums, home, den, gate)
    mixed = lax.all_to_all(mixed, LOCAL, 0, 0, tiled=True)
    return finish(place, x, mixed, *w_part, w_peer)[None]


def solution(mesh):
    parts = Mesh(mesh.devices.reshape(2, 4, 2, 8, 4), ("zh", "x", "c", "zl", "y"))
    return jax.shard_map(
        body,
        mesh=parts,
        in_specs=(
            P(USER, HIST, None),
            P(USER, HIST, None),
            P(USER, HIST, None),
            P(USER, None),
            P(USER, HIST),
            P(USER, HIST),
            P(USER, None),
            P(USER, None),
        ),
        out_specs=P(USER, HIST, None),
        check_vma=False,
    )
```

```python
import jax
import jax.numpy as jnp
from jax import lax
from jax.experimental import pallas as pl
from jax.experimental.pallas import tpu as pltpu
from jax.sharding import Mesh, PartitionSpec as P

D = 1024
HEADS = 8
HEAD = 128
BLOCK = 128
ROWS = 64
WIDE = D + 128
KV_ROWS = 1024
MY_ROWS = 576
HALF = 512
EVENTS = 2048
USER = ("zl", "y")
LOCAL = ("x", "c")
HIST = ("zh", "x", "c")
SCALE = HEAD ** (-0.5)
VMEM = pl.BlockSpec(memory_space=pltpu.VMEM)
ANY = pl.BlockSpec(memory_space=pl.ANY)
SMEM = pl.BlockSpec(memory_space=pltpu.SMEM)
PARAMS = pltpu.CompilerParams(vmem_limit_bytes=16 << 20)
WHOLE = pltpu.CompilerParams(vmem_limit_bytes=60 << 20)

def cost(megabytes):
    return pl.CostEstimate(flops=megabytes << 28, bytes_accessed=megabytes << 20, transcendentals=megabytes << 18)


C_PACKETS, C_GIVE, C_PROJECT, C_AWAY, C_OWN, C_MIX = 1, 1, 2000, 4, 4, 2000
F32 = jnp.float32
BF16 = jnp.bfloat16


def silu(v):
    h = v * 0.5
    return h + h * jnp.tanh(h)


def layer_norm(values):
    mean = jnp.mean(values, axis=-1, keepdims=True)
    centred = values - mean
    var = jnp.mean(centred * centred, axis=-1, keepdims=True)
    return centred * lax.rsqrt(var + 1e-05)


def swap(value, axis):
    return lax.ppermute(value, axis, [(0, 1), (1, 0)])


def along(value, axis, steps):
    return lax.ppermute(value, axis, [(i, (i + steps) % 4) for i in range(4)])


def columns_kernel(in_ref, out_w_ref, out_ref, block, sems):
    first = (lax.axis_index("x") * 2 + lax.axis_index("c")) * HEAD
    copies = []
    for part in range(5):
        ref, start = (in_ref, first + part * D) if part < 4 else (out_w_ref, first)
        at = pl.ds(pl.multiple_of(start, HEAD), HEAD)
        to = block.at[:, pl.ds(part * HEAD, HEAD)]
        copies.append(pltpu.make_async_copy(ref.at[:, at], to, sems.at[part]))
        copies[part].start()
    for copy in copies:
        copy.wait()
    for z in range(8):
        out_ref[z] = block[...]


def columns(*args):
    return pl.pallas_call(
        columns_kernel,
        name="columns",
        out_shape=jax.ShapeDtypeStruct((8, 32, 640), BF16),
        in_specs=[ANY, ANY],
        out_specs=VMEM,
        scratch_shapes=[pltpu.VMEM((32, 640), BF16), pltpu.SemaphoreType.DMA((5,))],
        compiler_params=WHOLE,
    )(*args)


def tags_of(owner_ref, user, cutoff):
    square = (ROWS, ROWS)
    diagonal = lax.broadcasted_iota(jnp.int32, square, 0) == lax.broadcasted_iota(jnp.int32, square, 1)
    before = jnp.zeros(user.shape, jnp.int32)
    for b in range(32):
        before = before + (owner_ref[0, b] < user).astype(jnp.int32)

    def column(row):
        spread_out = jnp.where(diagonal, jnp.broadcast_to(row.astype(F32), square), 0.0)
        return jnp.sum(spread_out, axis=1, keepdims=True)

    lane = lax.broadcasted_iota(jnp.int32, (ROWS, 128), 1)
    tags = jnp.where(lane == 0, column(before), 0.0)
    tags = jnp.where(lane == 1, column(cutoff >> 6), tags)
    return jnp.where(lane == 2, column(cutoff & 63), tags)


def packets_kernel(place_ref, owner_ref, x_ref, user_ref, cutoff_ref, k_ref, v_ref, *out_refs):
    normed = layer_norm(x_ref[...].astype(F32)).astype(BF16)
    tags = tags_of(owner_ref, user_ref[...], cutoff_ref[...]).astype(BF16)
    for s, ref in enumerate(out_refs):
        for core in range(2):
            start = ((place_ref[0] + s) & 3) * 256 + core * HEAD
            at = pl.ds(pl.multiple_of(start, HEAD), HEAD)
            ref[core * 256 : core * 256 + 256, :] = k_ref[:, at]
            ref[512 + core * 256 : 768 + core * 256, :] = v_ref[:, at]
        for part in range(8):
            to = KV_ROWS + part * ROWS
            ref[to : to + ROWS, :] = normed[:, part * HEAD : part * HEAD + HEAD]
        ref[KV_ROWS + 512 :, :] = tags


def packets(*args):
    return pl.pallas_call(
        packets_kernel,
        name="packets",
        out_shape=[jax.ShapeDtypeStruct((KV_ROWS + MY_ROWS, HEAD), BF16)] * 4,
        in_specs=[SMEM, SMEM] + [VMEM] * 5,
        out_specs=[VMEM] * 4,
        cost_estimate=cost(C_PACKETS),
        compiler_params=PARAMS,
    )(*args)


def give_kernel(place_ref, p0, p1, p2, p3, rows_ref, more_ref, kv_ref):
    other = 1 - place_ref[1]
    for s, ref in enumerate((p0, p1, p2, p3)):
        for i in range(2):
            at = pl.ds(pl.multiple_of(i * 512 + other * 256, 256), 256)
            kv_ref[s * 512 + i * 256 : s * 512 + i * 256 + 256, :] = ref[at, :]
        to = (rows_ref, more_ref)[s // 2]
        to[(s % 2) * MY_ROWS : (s % 2 + 1) * MY_ROWS, :] = ref[KV_ROWS:, :]


def give(*args):
    return pl.pallas_call(
        give_kernel,
        name="give",
        out_shape=[jax.ShapeDtypeStruct((n, HEAD), BF16) for n in (2 * MY_ROWS, 2 * MY_ROWS, 2048)],
        in_specs=[SMEM] + [VMEM] * 4,
        out_specs=[VMEM] * 3,
        cost_estimate=cost(C_GIVE),
        compiler_params=PARAMS,
    )(*args)


def out_part_kernel(w0, w1, w2, w3, after_ref, out_ref):
    for s, ref in enumerate((w0, w1, w2, w3)):
        out_ref[s] = ref[:, 512:]


def out_part(*args):
    return pl.pallas_call(
        out_part_kernel,
        name="out_part",
        out_shape=jax.ShapeDtypeStruct((4, 256, HEAD), BF16),
        in_specs=[VMEM] * 4 + [ANY],
        out_specs=VMEM,
        compiler_params=PARAMS,
    )(*args)


def stack_kernel(*refs):
    for s in range(4):
        refs[-1][s] = refs[s][...]


def stack(first, *rest):
    return pl.pallas_call(
        stack_kernel,
        name="stack",
        out_shape=jax.ShapeDtypeStruct((4,) + first.shape, BF16),
        in_specs=[VMEM] * 4 + [ANY] * (len(rest) - 3),
        out_specs=VMEM,
        compiler_params=PARAMS,
    )(first, *rest)


def load_weight(place_ref, w_refs, w_all, first, count):
    for s, ref in enumerate(w_refs):
        y = (place_ref[3] - s + 4) & 3
        for z in range(8):
            at = pl.ds(pl.multiple_of(z * 128 + y * 32, 32), 32)
            w_all[at, :] = ref[pl.ds(z * 32, 32), pl.ds(first, count)]


def load_rows(packet_refs, got_refs, rows):
    for s in range(4):
        got = (got_refs[s // 2], (s % 2) * MY_ROWS)
        for rel, (ref, first) in enumerate(((packet_refs[s], KV_ROWS), got)):
            for part in range(9):
                to, start = rel * 256 + s * ROWS, first + part * ROWS
                rows[to : to + ROWS, pl.ds(part * HEAD, HEAD)] = ref[start : start + ROWS, :]


def visible(tags):
    return tags[:, 0:1] * BLOCK, tags[:, 1:2] * 64.0 + tags[:, 2:3]


def project_kernel(
    place_ref, w0, w1, w2, w3, p0, p1, p2, p3, got, more,
    query_ref, gate_ref, den_ref, self_ref, rows, w_all,
):
    load_rows((p0, p1, p2, p3), (got, more), rows)
    load_weight(place_ref, (w0, w1, w2, w3), w_all, 0, 512)
    for i in range(2):
        at = pl.ds(i * 256, 256)
        proj = jnp.dot(rows[at, :D], w_all[...], preferred_element_type=F32)
        proj = silu(proj).astype(BF16)
        gate_ref[at, :] = proj[:, 0:128]
        query_ref[at, :] = proj[:, 256:384]
        query = proj[:, 256:384].astype(F32)
        score = jnp.sum(query * proj[:, 384:512].astype(F32), axis=-1, keepdims=True)
        self_ref[at, :] = silu(score * SCALE) * proj[:, 128:256].astype(F32)
    for i in range(4):
        at = pl.ds(i * 128, 128)
        tags = rows[at, D:].astype(F32)
        first, last = visible(tags)
        den_ref[at, :] = jnp.broadcast_to(last - first + 1.0, (128, HEAD))
        query_ref[HALF + i * 16 : HALF + i * 16 + 16, :] = tags.T[0:16, :].astype(BF16)


def project(*args):
    shape = (HALF, HEAD)
    return pl.pallas_call(
        project_kernel,
        name="project",
        out_shape=[
            jax.ShapeDtypeStruct((HALF + 64, HEAD), BF16),
            jax.ShapeDtypeStruct(shape, BF16),
            jax.ShapeDtypeStruct(shape, F32),
            jax.ShapeDtypeStruct(shape, F32),
        ],
        in_specs=[SMEM] + [VMEM] * 10,
        out_specs=[VMEM] * 4,
        scratch_shapes=[pltpu.VMEM((HALF, WIDE), BF16), pltpu.VMEM((D, 512), BF16)],
        cost_estimate=cost(C_PROJECT),
        compiler_params=PARAMS,
    )(*args)


def attend_kernel(place_ref, q_ref, p0, p1, p2, p3, kv_peer, plus_ref, out_ref):
    x, core, half = place_ref[0], place_ref[1], place_ref[2]
    event = lax.broadcasted_iota(jnp.int32, (256, 256), 1)
    for tile in range(2):
        at = pl.ds(tile * 256, 256)
        lows, counts = [], []
        for i in range(2):
            row = HALF + (tile * 2 + i) * 16
            tags = q_ref[row : row + 16, :].astype(F32)
            tags = jnp.concatenate([tags, jnp.zeros((112, 128), F32)], axis=0).T
            first, last = visible(tags)
            lows.append(first.astype(jnp.int32))
            counts.append((last - first).astype(jnp.uint32))
        low = jnp.broadcast_to(jnp.concatenate(lows, axis=0), (256, 256))
        count = jnp.broadcast_to(jnp.concatenate(counts, axis=0), (256, 256))
        query = q_ref[at, :]
        total = jnp.zeros((256, HEAD), F32)
        for s, pack in enumerate((p0, p1, p2, p3)):
            for rel, ref in enumerate((pack, kv_peer)):
                base = half * EVENTS + ((x - s + 4) & 3) * 512 + (core ^ rel) * 256
                row = s * 512 if rel else pl.multiple_of(core * 256, 256)
                keys, values = pl.ds(row, 256), pl.ds(row + (256 if rel else 512), 256)
                score = lax.dot_general(
                    query, ref[keys, :], (((1,), (1,)), ((), ())), preferred_element_type=F32
                )
                h = score * (0.5 * SCALE)
                w = h + h * jnp.tanh(h)
                seen = (event + base - low).astype(jnp.uint32) < count
                w = jnp.where(seen, w, 0.0).astype(BF16)
                total = total + jnp.dot(w, ref[values, :], preferred_element_type=F32)
        if out_ref.dtype == F32:
            total = total + plus_ref[at, :]
        out_ref[at, :] = total.astype(out_ref.dtype)


def attend(name, dtype, *args):
    return pl.pallas_call(
        attend_kernel,
        name=name,
        out_shape=jax.ShapeDtypeStruct((HALF, HEAD), dtype),
        in_specs=[SMEM] + [VMEM] * 7,
        out_specs=VMEM,
        cost_estimate=cost(C_AWAY if name == "other" else C_OWN),
        compiler_params=PARAMS,
    )(*args)


def mix_kernel(place_ref, sum_ref, home_ref, den_ref, gate_ref, out_ref):
    x, core = place_ref[0], place_ref[1]
    for rel in range(2):
        for s in range(4):
            at = pl.ds(rel * 256 + s * ROWS, ROWS)
            attended = (sum_ref[at, :] + home_ref[at, :].astype(F32)) / den_ref[at, :]
            mixed = layer_norm(attended) * gate_ref[at, :].astype(F32)
            out_ref[((x - s + 4) & 3) * 2 + (core ^ rel)] = mixed.astype(BF16)


def mix(*args):
    return pl.pallas_call(
        mix_kernel,
        name="mix",
        out_shape=jax.ShapeDtypeStruct((HEADS, ROWS, HEAD), BF16),
        in_specs=[SMEM] + [VMEM] * 4,
        out_specs=VMEM,
        cost_estimate=cost(C_MIX),
        compiler_params=PARAMS,
    )(*args)


def finish_kernel(place_ref, x_ref, mixed_ref, w0, w1, w2, w3, peer_ref, out_ref, by_line):
    along, core, line = place_ref[0], place_ref[1], place_ref[3]
    for y in range(4):
        for h in range(HEADS):
            by_line[y, :, h * 32 : h * 32 + 32] = mixed_ref[h, :, y * 32 : y * 32 + 32]
    left = jnp.concatenate([by_line[(line - step + 4) & 3] for step in range(4)], axis=1)
    for s, ref in enumerate((w0, w1, w2, w3)):
        for rel in range(2):
            at = ((along - s + 4) & 3) * 2 + (core ^ rel)
            at = pl.ds(pl.multiple_of(at * HEAD, HEAD), HEAD)
            right = (ref[...] if rel == 0 else peer_ref[s]).reshape(D, HEAD)
            projected = jnp.dot(left, right, preferred_element_type=F32)
            out_ref[:, at] = (x_ref[:, at].astype(F32) + projected).astype(BF16)


def finish(*args):
    return pl.pallas_call(
        finish_kernel,
        name="finish",
        out_shape=jax.ShapeDtypeStruct((ROWS, D), BF16),
        in_specs=[SMEM] + [VMEM] * 7,
        out_specs=VMEM,
        scratch_shapes=[pltpu.VMEM((4, ROWS, 256), BF16)],
        compiler_params=PARAMS,
    )(*args)


def body(cand_embed, hist_key, hist_value, block_owner, cand_user, cand_cutoff, w_in, w_out):
    x = cand_embed[0]
    place = [lax.axis_index(a) for a in ("x", "c", "zh", "y")]
    place = jnp.stack(place).astype(jnp.int32)

    cols = columns(w_in, w_out)
    cols = lax.all_to_all(cols, "zl", 0, 0, tiled=True).reshape(256, 640)
    cols = [along(cols, "y", s) if s else cols for s in range(4)]

    packs = packets(place, block_owner, x, cand_user, cand_cutoff, hist_key[0], hist_value[0])
    packs = [along(pack, "x", s) if s else pack for s, pack in enumerate(packs)]
    got, more, kv_peer = [swap(part, "c") for part in give(place, *packs)]

    query, gate, den, self_term = project(place, *cols, *packs, got, more)
    query_other = swap(query, "zh")

    w_part = out_part(*cols, query)
    w_part = [along(w_part, "x", s) if s else w_part for s in range(4)]

    away = attend("other", BF16, place, query_other, *packs, kv_peer, self_term)
    home = swap(away, "zh")
    sums = attend("own", F32, place, query, *packs, kv_peer, self_term)
    w_own = stack(*w_part, away)
    w_peer = swap(w_own, "c")

    mixed = mix(place, sums, home, den, gate)
    mixed = lax.all_to_all(mixed, LOCAL, 0, 0, tiled=True)
    return finish(place, x, mixed, *w_part, w_peer)[None]


def solution(mesh):
    parts = Mesh(mesh.devices.reshape(2, 4, 2, 8, 4), ("zh", "x", "c", "zl", "y"))
    return jax.shard_map(
        body,
        mesh=parts,
        in_specs=(
            P(USER, HIST, None),
            P(USER, HIST, None),
            P(USER, HIST, None),
            P(USER, None),
            P(USER, HIST),
            P(USER, HIST),
            P(USER, None),
            P(USER, None),
        ),
        out_specs=P(USER, HIST, None),
        check_vma=False,
    )
```

```python
import jax
import jax.numpy as jnp
from jax import lax
from jax.experimental import pallas as pl
from jax.experimental.pallas import tpu as pltpu
from jax.sharding import Mesh, PartitionSpec as P

D = 1024
HEADS = 8
HEAD = 128
BLOCK = 128
ROWS = 64
WIDE = D + 128
KV_ROWS = 1024
MY_ROWS = 576
HALF = 512
EVENTS = 2048
USER = ("zl", "y")
LOCAL = ("x", "c")
HIST = ("zh", "x", "c")
SCALE = HEAD ** (-0.5)
VMEM = pl.BlockSpec(memory_space=pltpu.VMEM)
ANY = pl.BlockSpec(memory_space=pl.ANY)
SMEM = pl.BlockSpec(memory_space=pltpu.SMEM)
PARAMS = pltpu.CompilerParams(vmem_limit_bytes=16 << 20)
WHOLE = pltpu.CompilerParams(vmem_limit_bytes=60 << 20)

def cost(megabytes):
    return pl.CostEstimate(flops=megabytes << 28, bytes_accessed=megabytes << 20, transcendentals=megabytes << 18)


C_PACKETS, C_GIVE, C_PROJECT, C_AWAY, C_OWN, C_MIX = 1, 1, 2000, 4, 4, 2000
F32 = jnp.float32
BF16 = jnp.bfloat16


def silu(v):
    h = v * 0.5
    return h + h * jnp.tanh(h)


def layer_norm(values):
    mean = jnp.mean(values, axis=-1, keepdims=True)
    centred = values - mean
    var = jnp.mean(centred * centred, axis=-1, keepdims=True)
    return centred * lax.rsqrt(var + 1e-05)


def swap(value, axis):
    return lax.ppermute(value, axis, [(0, 1), (1, 0)])


def along(value, axis, steps):
    return lax.ppermute(value, axis, [(i, (i + steps) % 4) for i in range(4)])


def columns_kernel(in_ref, out_w_ref, out_ref, block, sems, out_sems):
    first = (lax.axis_index("x") * 2 + lax.axis_index("c")) * HEAD
    copies = []
    for part in range(5):
        ref, start = (in_ref, first + part * D) if part < 4 else (out_w_ref, first)
        at = pl.ds(pl.multiple_of(start, HEAD), HEAD)
        to = block.at[:, pl.ds(part * HEAD, HEAD)]
        copies.append(pltpu.make_async_copy(ref.at[:, at], to, sems.at[part]))
        copies[part].start()
    for copy in copies:
        copy.wait()
    copies = [pltpu.make_async_copy(block, out_ref.at[z], out_sems.at[z]) for z in range(8)]
    for copy in copies:
        copy.start()
    for copy in copies:
        copy.wait()


def columns(*args):
    return pl.pallas_call(
        columns_kernel,
        name="columns",
        out_shape=jax.ShapeDtypeStruct((8, 32, 640), BF16),
        in_specs=[ANY, ANY],
        out_specs=ANY,
        scratch_shapes=[
            pltpu.VMEM((32, 640), BF16),
            pltpu.SemaphoreType.DMA((5,)),
            pltpu.SemaphoreType.DMA((8,)),
        ],
        compiler_params=WHOLE,
    )(*args)


def tags_of(owner_ref, user, cutoff):
    square = (ROWS, ROWS)
    diagonal = lax.broadcasted_iota(jnp.int32, square, 0) == lax.broadcasted_iota(jnp.int32, square, 1)
    before = jnp.zeros(user.shape, jnp.int32)
    for b in range(32):
        before = before + (owner_ref[0, b] < user).astype(jnp.int32)

    def column(row):
        spread_out = jnp.where(diagonal, jnp.broadcast_to(row.astype(F32), square), 0.0)
        return jnp.sum(spread_out, axis=1, keepdims=True)

    lane = lax.broadcasted_iota(jnp.int32, (ROWS, 128), 1)
    tags = jnp.where(lane == 0, column(before), 0.0)
    tags = jnp.where(lane == 1, column(cutoff >> 6), tags)
    return jnp.where(lane == 2, column(cutoff & 63), tags)


def packets_kernel(place_ref, owner_ref, x_ref, user_ref, cutoff_ref, k_ref, v_ref, *out_refs):
    normed = layer_norm(x_ref[...].astype(F32)).astype(BF16)
    tags = tags_of(owner_ref, user_ref[...], cutoff_ref[...]).astype(BF16)
    for s, ref in enumerate(out_refs):
        for core in range(2):
            start = ((place_ref[0] + s) & 3) * 256 + core * HEAD
            at = pl.ds(pl.multiple_of(start, HEAD), HEAD)
            ref[core * 256 : core * 256 + 256, :] = k_ref[:, at]
            ref[512 + core * 256 : 768 + core * 256, :] = v_ref[:, at]
        for part in range(8):
            to = KV_ROWS + part * ROWS
            ref[to : to + ROWS, :] = normed[:, part * HEAD : part * HEAD + HEAD]
        ref[KV_ROWS + 512 :, :] = tags


def packets(*args):
    return pl.pallas_call(
        packets_kernel,
        name="packets",
        out_shape=[jax.ShapeDtypeStruct((KV_ROWS + MY_ROWS, HEAD), BF16)] * 4,
        in_specs=[SMEM, SMEM] + [VMEM] * 5,
        out_specs=[VMEM] * 4,
        cost_estimate=cost(C_PACKETS),
        compiler_params=PARAMS,
    )(*args)


def give_kernel(place_ref, p0, p1, p2, p3, rows_ref, more_ref, kv_ref):
    other = 1 - place_ref[1]
    for s, ref in enumerate((p0, p1, p2, p3)):
        for i in range(2):
            at = pl.ds(pl.multiple_of(i * 512 + other * 256, 256), 256)
            kv_ref[s * 512 + i * 256 : s * 512 + i * 256 + 256, :] = ref[at, :]
        to = (rows_ref, more_ref)[s // 2]
        to[(s % 2) * MY_ROWS : (s % 2 + 1) * MY_ROWS, :] = ref[KV_ROWS:, :]


def give(*args):
    return pl.pallas_call(
        give_kernel,
        name="give",
        out_shape=[jax.ShapeDtypeStruct((n, HEAD), BF16) for n in (2 * MY_ROWS, 2 * MY_ROWS, 2048)],
        in_specs=[SMEM] + [VMEM] * 4,
        out_specs=[VMEM] * 3,
        cost_estimate=cost(C_GIVE),
        compiler_params=PARAMS,
    )(*args)


def rows_kernel(p0, p1, p2, p3, got, more, rows):
    load_rows((p0, p1, p2, p3), (got, more), rows)


def assemble(*args):
    return pl.pallas_call(
        rows_kernel,
        name="assemble",
        out_shape=jax.ShapeDtypeStruct((HALF, WIDE), BF16),
        in_specs=[VMEM] * 6,
        out_specs=VMEM,
        compiler_params=PARAMS,
    )(*args)


def stack_kernel(*refs):
    for s in range(4):
        refs[-1][s] = refs[s][...]


def stack(first, *rest):
    return pl.pallas_call(
        stack_kernel,
        name="stack",
        out_shape=jax.ShapeDtypeStruct((4,) + first.shape, BF16),
        in_specs=[VMEM] * 4 + [ANY] * (len(rest) - 3),
        out_specs=VMEM,
        compiler_params=PARAMS,
    )(first, *rest)


def load_weight(place_ref, w_refs, w_all, first, count):
    for s, ref in enumerate(w_refs):
        y = (place_ref[3] - s + 4) & 3
        for z in range(8):
            at = pl.ds(pl.multiple_of(z * 128 + y * 32, 32), 32)
            w_all[at, :] = ref[pl.ds(z * 32, 32), pl.ds(first, count)]


def load_rows(packet_refs, got_refs, rows):
    for s in range(4):
        got = (got_refs[s // 2], (s % 2) * MY_ROWS)
        for rel, (ref, first) in enumerate(((packet_refs[s], KV_ROWS), got)):
            for part in range(9):
                to, start = rel * 256 + s * ROWS, first + part * ROWS
                rows[to : to + ROWS, pl.ds(part * HEAD, HEAD)] = ref[start : start + ROWS, :]


def visible(tags):
    return tags[:, 0:1] * BLOCK, tags[:, 1:2] * 64.0 + tags[:, 2:3]


def project_kernel(
    place_ref, w0, w1, w2, w3, rows, query_ref, gate_ref, den_ref, self_ref, part_ref, w_all
):
    for s, ref in enumerate((w0, w1, w2, w3)):
        part_ref[(place_ref[3] - s + 4) & 3] = ref[:, 512:]
    load_weight(place_ref, (w0, w1, w2, w3), w_all, 0, 512)
    for i in range(2):
        at = pl.ds(i * 256, 256)
        proj = jnp.dot(rows[at, :D], w_all[...], preferred_element_type=F32)
        proj = silu(proj).astype(BF16)
        gate_ref[at, :] = proj[:, 0:128]
        query_ref[at, :] = proj[:, 256:384]
        query = proj[:, 256:384].astype(F32)
        score = jnp.sum(query * proj[:, 384:512].astype(F32), axis=-1, keepdims=True)
        self_ref[at, :] = silu(score * SCALE) * proj[:, 128:256].astype(F32)
    for i in range(4):
        at = pl.ds(i * 128, 128)
        tags = rows[at, D:].astype(F32)
        first, last = visible(tags)
        den_ref[at, :] = jnp.broadcast_to(last - first + 1.0, (128, HEAD))
        query_ref[HALF + i * 16 : HALF + i * 16 + 16, :] = tags.T[0:16, :].astype(BF16)


def project(*args):
    shape = (HALF, HEAD)
    return pl.pallas_call(
        project_kernel,
        name="project",
        out_shape=[
            jax.ShapeDtypeStruct((HALF + 64, HEAD), BF16),
            jax.ShapeDtypeStruct(shape, BF16),
            jax.ShapeDtypeStruct(shape, F32),
            jax.ShapeDtypeStruct(shape, F32),
            jax.ShapeDtypeStruct((4, 256, HEAD), BF16),
        ],
        in_specs=[SMEM] + [VMEM] * 5,
        out_specs=[VMEM] * 5,
        scratch_shapes=[pltpu.VMEM((D, 512), BF16)],
        cost_estimate=cost(C_PROJECT),
        compiler_params=PARAMS,
    )(*args)


def attend_kernel(place_ref, q_ref, p0, p1, p2, p3, kv_peer, plus_ref, out_ref, kv_all, sem):
    x, core, half = place_ref[0], place_ref[1], place_ref[2]
    copy = pltpu.make_async_copy(kv_peer, kv_all, sem)
    copy.start()
    event = lax.broadcasted_iota(jnp.int32, (256, 256), 1)
    for tile in range(2):
        at = pl.ds(tile * 256, 256)
        lows, counts = [], []
        for i in range(2):
            row = HALF + (tile * 2 + i) * 16
            tags = q_ref[row : row + 16, :].astype(F32)
            tags = jnp.concatenate([tags, jnp.zeros((112, 128), F32)], axis=0).T
            first, last = visible(tags)
            lows.append(first.astype(jnp.int32))
            counts.append((last - first).astype(jnp.uint32))
        low = jnp.broadcast_to(jnp.concatenate(lows, axis=0), (256, 256))
        count = jnp.broadcast_to(jnp.concatenate(counts, axis=0), (256, 256))
        query = q_ref[at, :]
        total = jnp.zeros((256, HEAD), F32)
        for rel in range(2):
            if tile == 0 and rel:
                copy.wait()
            for s, pack in enumerate((p0, p1, p2, p3)):
                base = half * EVENTS + ((x - s + 4) & 3) * 512 + (core ^ rel) * 256
                row = s * 512 if rel else pl.multiple_of(core * 256, 256)
                keys, values = pl.ds(row, 256), pl.ds(row + (256 if rel else 512), 256)
                ref = kv_all if rel else pack
                score = lax.dot_general(
                    query, ref[keys, :], (((1,), (1,)), ((), ())), preferred_element_type=F32
                )
                h = score * (0.5 * SCALE)
                w = h + h * jnp.tanh(h)
                seen = (event + base - low).astype(jnp.uint32) < count
                w = jnp.where(seen, w, 0.0).astype(BF16)
                total = total + jnp.dot(w, ref[values, :], preferred_element_type=F32)
        if out_ref.dtype == F32:
            total = total + plus_ref[at, :]
        out_ref[at, :] = total.astype(out_ref.dtype)


def attend(name, dtype, *args):
    return pl.pallas_call(
        attend_kernel,
        name=name,
        out_shape=jax.ShapeDtypeStruct((HALF, HEAD), dtype),
        in_specs=[SMEM] + [VMEM] * 5 + [ANY, VMEM],
        out_specs=VMEM,
        scratch_shapes=[pltpu.VMEM((2048, HEAD), BF16), pltpu.SemaphoreType.DMA],
        cost_estimate=cost(C_AWAY if name == "other" else C_OWN),
        compiler_params=PARAMS,
    )(*args)


def mix_kernel(place_ref, sum_ref, home_ref, den_ref, gate_ref, out_ref):
    x, core = place_ref[0], place_ref[1]
    for rel in range(2):
        for s in range(4):
            at = pl.ds(rel * 256 + s * ROWS, ROWS)
            attended = (sum_ref[at, :] + home_ref[at, :].astype(F32)) / den_ref[at, :]
            mixed = layer_norm(attended) * gate_ref[at, :].astype(F32)
            out_ref[((x - s + 4) & 3) * 2 + (core ^ rel)] = mixed.astype(BF16)


def mix(*args):
    return pl.pallas_call(
        mix_kernel,
        name="mix",
        out_shape=jax.ShapeDtypeStruct((HEADS, ROWS, HEAD), BF16),
        in_specs=[SMEM] + [VMEM] * 4,
        out_specs=VMEM,
        cost_estimate=cost(C_MIX),
        compiler_params=PARAMS,
    )(*args)


def finish_kernel(place_ref, x_ref, mixed_ref, w0, w1, w2, w3, peer_ref, out_ref):
    along, core = place_ref[0], place_ref[1]
    pieces = [mixed_ref[h, :, y * 32 : y * 32 + 32] for y in range(4) for h in range(HEADS)]
    left = jnp.concatenate(pieces, axis=1)
    for s, ref in enumerate((w0, w1, w2, w3)):
        for rel in range(2):
            at = ((along - s + 4) & 3) * 2 + (core ^ rel)
            at = pl.ds(pl.multiple_of(at * HEAD, HEAD), HEAD)
            right = (ref[...] if rel == 0 else peer_ref[s]).reshape(D, HEAD)
            projected = jnp.dot(left, right, preferred_element_type=F32)
            out_ref[:, at] = (x_ref[:, at].astype(F32) + projected).astype(BF16)


def finish(*args):
    return pl.pallas_call(
        finish_kernel,
        name="finish",
        out_shape=jax.ShapeDtypeStruct((ROWS, D), BF16),
        in_specs=[SMEM] + [VMEM] * 7,
        out_specs=VMEM,
        compiler_params=PARAMS,
    )(*args)


def body(cand_embed, hist_key, hist_value, block_owner, cand_user, cand_cutoff, w_in, w_out):
    x = cand_embed[0]
    place = [lax.axis_index(a) for a in ("x", "c", "zh", "y")]
    place = jnp.stack(place).astype(jnp.int32)

    cols = columns(w_in, w_out)
    cols = lax.all_to_all(cols, "zl", 0, 0, tiled=True).reshape(256, 640)
    cols = [along(cols, "y", s) if s else cols for s in range(4)]

    packs = packets(place, block_owner, x, cand_user, cand_cutoff, hist_key[0], hist_value[0])
    packs = [along(pack, "x", s) if s else pack for s, pack in enumerate(packs)]
    got, more, kv_peer = [swap(part, "c") for part in give(place, *packs)]

    rows = assemble(*packs, got, more)
    query, gate, den, self_term, w_part = project(place, *cols, rows)
    query_other = swap(query, "zh")
    w_part = [along(w_part, "x", s) if s else w_part for s in range(4)]

    away = attend("other", BF16, place, query_other, *packs, kv_peer, self_term)
    home = swap(away, "zh")
    sums = attend("own", F32, place, query, *packs, kv_peer, self_term)
    w_own = stack(*w_part, away)
    w_peer = swap(w_own, "c")

    mixed = mix(place, sums, home, den, gate)
    mixed = lax.all_to_all(mixed, LOCAL, 0, 0, tiled=True)
    return finish(place, x, mixed, *w_part, w_peer)[None]


def solution(mesh):
    parts = Mesh(mesh.devices.reshape(2, 4, 2, 8, 4), ("zh", "x", "c", "zl", "y"))
    return jax.shard_map(
        body,
        mesh=parts,
        in_specs=(
            P(USER, HIST, None),
            P(USER, HIST, None),
            P(USER, HIST, None),
            P(USER, None),
            P(USER, HIST),
            P(USER, HIST),
            P(USER, None),
            P(USER, None),
        ),
        out_specs=P(USER, HIST, None),
        check_vma=False,
    )
```

```python
import jax
import jax.numpy as jnp
from jax import lax
from jax.experimental import pallas as pl
from jax.experimental.pallas import tpu as pltpu
from jax.sharding import Mesh, PartitionSpec as P

D = 1024
HEADS = 8
HEAD = 128
BLOCK = 128
ROWS = 64
WIDE = D + 128
KV_ROWS = 1024
MY_ROWS = 576
HALF = 512
EVENTS = 2048
USER = ("zl", "y")
LOCAL = ("x", "c")
HIST = ("zh", "x", "c")
SCALE = HEAD ** (-0.5)
VMEM = pl.BlockSpec(memory_space=pltpu.VMEM)
ANY = pl.BlockSpec(memory_space=pl.ANY)
SMEM = pl.BlockSpec(memory_space=pltpu.SMEM)
PARAMS = pltpu.CompilerParams(vmem_limit_bytes=16 << 20)
WHOLE = pltpu.CompilerParams(vmem_limit_bytes=60 << 20)

def cost(megabytes):
    return pl.CostEstimate(flops=megabytes << 28, bytes_accessed=megabytes << 20, transcendentals=megabytes << 18)


C_PACKETS, C_GIVE, C_PROJECT, C_AWAY, C_OWN, C_MIX = 1, 1, 2000, 4, 4, 2000
F32 = jnp.float32
BF16 = jnp.bfloat16


def silu(v):
    h = v * 0.5
    return h + h * jnp.tanh(h)


def layer_norm(values):
    mean = jnp.mean(values, axis=-1, keepdims=True)
    centred = values - mean
    var = jnp.mean(centred * centred, axis=-1, keepdims=True)
    return centred * lax.rsqrt(var + 1e-05)


def swap(value, axis):
    return lax.ppermute(value, axis, [(0, 1), (1, 0)])


def along(value, axis, steps):
    return lax.ppermute(value, axis, [(i, (i + steps) % 4) for i in range(4)])


def columns_kernel(in_ref, out_w_ref, out_ref, block, sems, out_sems):
    first = (lax.axis_index("x") * 2 + lax.axis_index("c")) * HEAD
    copies = []
    for part in range(5):
        ref, start = (in_ref, first + part * D) if part < 4 else (out_w_ref, first)
        at = pl.ds(pl.multiple_of(start, HEAD), HEAD)
        to = block.at[:, pl.ds(part * HEAD, HEAD)]
        copies.append(pltpu.make_async_copy(ref.at[:, at], to, sems.at[part]))
        copies[part].start()
    for copy in copies:
        copy.wait()
    copies = [pltpu.make_async_copy(block, out_ref.at[z], out_sems.at[z]) for z in range(8)]
    for copy in copies:
        copy.start()
    for copy in copies:
        copy.wait()


def columns(*args):
    return pl.pallas_call(
        columns_kernel,
        name="columns",
        out_shape=jax.ShapeDtypeStruct((8, 32, 640), BF16),
        in_specs=[ANY, ANY],
        out_specs=ANY,
        scratch_shapes=[
            pltpu.VMEM((32, 640), BF16),
            pltpu.SemaphoreType.DMA((5,)),
            pltpu.SemaphoreType.DMA((8,)),
        ],
        compiler_params=WHOLE,
    )(*args)


def tags_of(owner_ref, user, cutoff):
    square = (ROWS, ROWS)
    diagonal = lax.broadcasted_iota(jnp.int32, square, 0) == lax.broadcasted_iota(jnp.int32, square, 1)
    before = jnp.zeros(user.shape, jnp.int32)
    for b in range(32):
        before = before + (owner_ref[0, b] < user).astype(jnp.int32)

    def column(row):
        spread_out = jnp.where(diagonal, jnp.broadcast_to(row.astype(F32), square), 0.0)
        return jnp.sum(spread_out, axis=1, keepdims=True)

    lane = lax.broadcasted_iota(jnp.int32, (ROWS, 128), 1)
    tags = jnp.where(lane == 0, column(before), 0.0)
    tags = jnp.where(lane == 1, column(cutoff >> 6), tags)
    return jnp.where(lane == 2, column(cutoff & 63), tags)


def packets_kernel(place_ref, owner_ref, x_ref, user_ref, cutoff_ref, k_ref, v_ref, *out_refs):
    normed = layer_norm(x_ref[...].astype(F32)).astype(BF16)
    tags = tags_of(owner_ref, user_ref[...], cutoff_ref[...]).astype(BF16)
    for s, ref in enumerate(out_refs):
        for core in range(2):
            start = ((place_ref[0] + s) & 3) * 256 + core * HEAD
            at = pl.ds(pl.multiple_of(start, HEAD), HEAD)
            ref[core * 256 : core * 256 + 256, :] = k_ref[:, at]
            ref[512 + core * 256 : 768 + core * 256, :] = v_ref[:, at]
        for part in range(8):
            to = KV_ROWS + part * ROWS
            ref[to : to + ROWS, :] = normed[:, part * HEAD : part * HEAD + HEAD]
        ref[KV_ROWS + 512 :, :] = tags


def packets(*args):
    return pl.pallas_call(
        packets_kernel,
        name="packets",
        out_shape=[jax.ShapeDtypeStruct((KV_ROWS + MY_ROWS, HEAD), BF16)] * 4,
        in_specs=[SMEM, SMEM] + [VMEM] * 5,
        out_specs=[VMEM] * 4,
        cost_estimate=cost(C_PACKETS),
        compiler_params=PARAMS,
    )(*args)


def give_kernel(place_ref, p0, p1, p2, p3, rows_ref, more_ref, kv_ref):
    other = 1 - place_ref[1]
    for s, ref in enumerate((p0, p1, p2, p3)):
        for i in range(2):
            at = pl.ds(pl.multiple_of(i * 512 + other * 256, 256), 256)
            kv_ref[s * 512 + i * 256 : s * 512 + i * 256 + 256, :] = ref[at, :]
        to = (rows_ref, more_ref)[s // 2]
        to[(s % 2) * MY_ROWS : (s % 2 + 1) * MY_ROWS, :] = ref[KV_ROWS:, :]


def give(*args):
    return pl.pallas_call(
        give_kernel,
        name="give",
        out_shape=[jax.ShapeDtypeStruct((n, HEAD), BF16) for n in (2 * MY_ROWS, 2 * MY_ROWS, 2048)],
        in_specs=[SMEM] + [VMEM] * 4,
        out_specs=[VMEM] * 3,
        cost_estimate=cost(C_GIVE),
        compiler_params=PARAMS,
    )(*args)


def rows_kernel(p0, p1, p2, p3, got, more, rows):
    load_rows((p0, p1, p2, p3), (got, more), rows)


def assemble(*args):
    return pl.pallas_call(
        rows_kernel,
        name="assemble",
        out_shape=jax.ShapeDtypeStruct((HALF, WIDE), BF16),
        in_specs=[VMEM] * 6,
        out_specs=VMEM,
        compiler_params=PARAMS,
    )(*args)


def stack_kernel(*refs):
    for s in range(4):
        refs[-1][s] = refs[s][...]


def stack(first, *rest):
    return pl.pallas_call(
        stack_kernel,
        name="stack",
        out_shape=jax.ShapeDtypeStruct((4,) + first.shape, BF16),
        in_specs=[VMEM] * 4 + [ANY] * (len(rest) - 3),
        out_specs=VMEM,
        compiler_params=PARAMS,
    )(first, *rest)


def load_weight(place_ref, w_refs, w_all, first, count):
    for s, ref in enumerate(w_refs):
        y = (place_ref[3] - s + 4) & 3
        for z in range(8):
            at = pl.ds(pl.multiple_of(z * 128 + y * 32, 32), 32)
            w_all[at, :] = ref[pl.ds(z * 32, 32), pl.ds(first, count)]


def load_rows(packet_refs, got_refs, rows):
    for s in range(4):
        got = (got_refs[s // 2], (s % 2) * MY_ROWS)
        for rel, (ref, first) in enumerate(((packet_refs[s], KV_ROWS), got)):
            for part in range(9):
                to, start = rel * 256 + s * ROWS, first + part * ROWS
                rows[to : to + ROWS, pl.ds(part * HEAD, HEAD)] = ref[start : start + ROWS, :]


def visible(tags):
    return tags[:, 0:1] * BLOCK, tags[:, 1:2] * 64.0 + tags[:, 2:3]


def project_kernel(
    place_ref, w0, w1, w2, w3, rows, query_ref, gate_ref, den_ref, self_ref, part_ref, w_all
):
    for s, ref in enumerate((w0, w1, w2, w3)):
        part_ref[(place_ref[3] - s + 4) & 3] = ref[:, 512:]
    load_weight(place_ref, (w0, w1, w2, w3), w_all, 0, 512)
    for i in range(2):
        at = pl.ds(i * 256, 256)
        proj = jnp.dot(rows[at, :D], w_all[...], preferred_element_type=F32)
        proj = silu(proj).astype(BF16)
        gate_ref[at, :] = proj[:, 0:128]
        query_ref[at, :] = proj[:, 256:384]
        query = proj[:, 256:384].astype(F32)
        score = jnp.sum(query * proj[:, 384:512].astype(F32), axis=-1, keepdims=True)
        self_ref[at, :] = silu(score * SCALE) * proj[:, 128:256].astype(F32)
    labels = []
    for i in range(4):
        at = pl.ds(i * 128, 128)
        tags = rows[at, D:].astype(F32)
        first, last = visible(tags)
        den_ref[at, :] = jnp.broadcast_to(last - first + 1.0, (128, HEAD))
        labels.append(tags.T[0:4, :])
    query_ref[HALF:, :] = jnp.concatenate(labels, axis=0).astype(BF16)


def project(*args):
    shape = (HALF, HEAD)
    return pl.pallas_call(
        project_kernel,
        name="project",
        out_shape=[
            jax.ShapeDtypeStruct((HALF + 16, HEAD), BF16),
            jax.ShapeDtypeStruct(shape, BF16),
            jax.ShapeDtypeStruct(shape, F32),
            jax.ShapeDtypeStruct(shape, F32),
            jax.ShapeDtypeStruct((4, 256, HEAD), BF16),
        ],
        in_specs=[SMEM] + [VMEM] * 5,
        out_specs=[VMEM] * 5,
        scratch_shapes=[pltpu.VMEM((D, 512), BF16)],
        cost_estimate=cost(C_PROJECT),
        compiler_params=PARAMS,
    )(*args)


def attend_kernel(place_ref, q_ref, p0, p1, p2, p3, kv_peer, plus_ref, out_ref, kv_all, sem):
    x, core, half = place_ref[0], place_ref[1], place_ref[2]
    copy = pltpu.make_async_copy(kv_peer, kv_all, sem)
    copy.start()
    event = lax.broadcasted_iota(jnp.int32, (256, 256), 1)
    labels = q_ref[HALF : HALF + 16, :].astype(F32)
    for tile in range(2):
        at = pl.ds(tile * 256, 256)
        lows, counts = [], []
        for i in range(2):
            row = (tile * 2 + i) * 4
            tags = labels[row : row + 4, :]
            tags = jnp.concatenate([tags, jnp.zeros((124, 128), F32)], axis=0).T
            first, last = visible(tags)
            lows.append(first.astype(jnp.int32))
            counts.append((last - first).astype(jnp.uint32))
        low = jnp.broadcast_to(jnp.concatenate(lows, axis=0), (256, 256))
        count = jnp.broadcast_to(jnp.concatenate(counts, axis=0), (256, 256))
        query = q_ref[at, :]
        total = jnp.zeros((256, HEAD), F32)
        for rel in range(2):
            if tile == 0 and rel:
                copy.wait()
            for s, pack in enumerate((p0, p1, p2, p3)):
                base = half * EVENTS + ((x - s + 4) & 3) * 512 + (core ^ rel) * 256
                row = s * 512 if rel else pl.multiple_of(core * 256, 256)
                keys, values = pl.ds(row, 256), pl.ds(row + (256 if rel else 512), 256)
                ref = kv_all if rel else pack
                score = lax.dot_general(
                    query, ref[keys, :], (((1,), (1,)), ((), ())), preferred_element_type=F32
                )
                h = score * (0.5 * SCALE)
                w = h + h * jnp.tanh(h)
                seen = (event + base - low).astype(jnp.uint32) < count
                w = jnp.where(seen, w, 0.0).astype(BF16)
                total = total + jnp.dot(w, ref[values, :], preferred_element_type=F32)
        if out_ref.dtype == F32:
            total = total + plus_ref[at, :]
        out_ref[at, :] = total.astype(out_ref.dtype)


def attend(name, dtype, *args):
    return pl.pallas_call(
        attend_kernel,
        name=name,
        out_shape=jax.ShapeDtypeStruct((HALF, HEAD), dtype),
        in_specs=[SMEM] + [VMEM] * 5 + [ANY, VMEM],
        out_specs=VMEM,
        scratch_shapes=[pltpu.VMEM((2048, HEAD), BF16), pltpu.SemaphoreType.DMA],
        cost_estimate=cost(C_AWAY if name == "other" else C_OWN),
        compiler_params=PARAMS,
    )(*args)


def mix_kernel(place_ref, sum_ref, home_ref, den_ref, gate_ref, out_ref):
    x, core = place_ref[0], place_ref[1]
    for rel in range(2):
        for s in range(4):
            at = pl.ds(rel * 256 + s * ROWS, ROWS)
            attended = (sum_ref[at, :] + home_ref[at, :].astype(F32)) / den_ref[at, :]
            mixed = layer_norm(attended) * gate_ref[at, :].astype(F32)
            out_ref[((x - s + 4) & 3) * 2 + (core ^ rel)] = mixed.astype(BF16)


def mix(*args):
    return pl.pallas_call(
        mix_kernel,
        name="mix",
        out_shape=jax.ShapeDtypeStruct((HEADS, ROWS, HEAD), BF16),
        in_specs=[SMEM] + [VMEM] * 4,
        out_specs=VMEM,
        cost_estimate=cost(C_MIX),
        compiler_params=PARAMS,
    )(*args)


def finish_kernel(place_ref, x_ref, mixed_ref, w0, w1, w2, w3, peer_ref, out_ref):
    along, core = place_ref[0], place_ref[1]
    pieces = [mixed_ref[h, :, y * 32 : y * 32 + 32] for y in range(4) for h in range(HEADS)]
    left = jnp.concatenate(pieces, axis=1)
    for s, ref in enumerate((w0, w1, w2, w3)):
        for rel in range(2):
            at = ((along - s + 4) & 3) * 2 + (core ^ rel)
            at = pl.ds(pl.multiple_of(at * HEAD, HEAD), HEAD)
            right = (ref[...] if rel == 0 else peer_ref[s]).reshape(D, HEAD)
            projected = jnp.dot(left, right, preferred_element_type=F32)
            out_ref[:, at] = (x_ref[:, at].astype(F32) + projected).astype(BF16)


def finish(*args):
    return pl.pallas_call(
        finish_kernel,
        name="finish",
        out_shape=jax.ShapeDtypeStruct((ROWS, D), BF16),
        in_specs=[SMEM] + [VMEM] * 7,
        out_specs=VMEM,
        compiler_params=PARAMS,
    )(*args)


def body(cand_embed, hist_key, hist_value, block_owner, cand_user, cand_cutoff, w_in, w_out):
    x = cand_embed[0]
    place = [lax.axis_index(a) for a in ("x", "c", "zh", "y")]
    place = jnp.stack(place).astype(jnp.int32)

    cols = columns(w_in, w_out)
    cols = lax.all_to_all(cols, "zl", 0, 0, tiled=True).reshape(256, 640)
    cols = [along(cols, "y", s) if s else cols for s in range(4)]

    packs = packets(place, block_owner, x, cand_user, cand_cutoff, hist_key[0], hist_value[0])
    packs = [along(pack, "x", s) if s else pack for s, pack in enumerate(packs)]
    got, more, kv_peer = [swap(part, "c") for part in give(place, *packs)]

    rows = assemble(*packs, got, more)
    query, gate, den, self_term, w_part = project(place, *cols, rows)
    query_other = swap(query, "zh")
    w_part = [along(w_part, "x", s) if s else w_part for s in range(4)]

    away = attend("other", BF16, place, query_other, *packs, kv_peer, self_term)
    home = swap(away, "zh")
    sums = attend("own", F32, place, query, *packs, kv_peer, self_term)
    w_own = stack(*w_part, away)
    w_peer = swap(w_own, "c")

    mixed = mix(place, sums, home, den, gate)
    mixed = lax.all_to_all(mixed, LOCAL, 0, 0, tiled=True)
    return finish(place, x, mixed, *w_part, w_peer)[None]


def solution(mesh):
    parts = Mesh(mesh.devices.reshape(2, 4, 2, 8, 4), ("zh", "x", "c", "zl", "y"))
    return jax.shard_map(
        body,
        mesh=parts,
        in_specs=(
            P(USER, HIST, None),
            P(USER, HIST, None),
            P(USER, HIST, None),
            P(USER, None),
            P(USER, HIST),
            P(USER, HIST),
            P(USER, None),
            P(USER, None),
        ),
        out_specs=P(USER, HIST, None),
        check_vma=False,
    )
```

```python
import jax
import jax.numpy as jnp
from jax import lax
from jax.experimental import pallas as pl
from jax.experimental.pallas import tpu as pltpu
from jax.sharding import Mesh, PartitionSpec as P

D = 1024
HEADS = 8
HEAD = 128
BLOCK = 128
ROWS = 64
WIDE = D + 128
KV_ROWS = 1024
MY_ROWS = 576
HALF = 512
EVENTS = 2048
USER = ("zl", "y")
LOCAL = ("x", "c")
HIST = ("zh", "x", "c")
SCALE = HEAD ** (-0.5)
VMEM = pl.BlockSpec(memory_space=pltpu.VMEM)
ANY = pl.BlockSpec(memory_space=pl.ANY)
SMEM = pl.BlockSpec(memory_space=pltpu.SMEM)
PARAMS = pltpu.CompilerParams(vmem_limit_bytes=16 << 20)
WHOLE = pltpu.CompilerParams(vmem_limit_bytes=60 << 20)

def cost(megabytes):
    return pl.CostEstimate(flops=megabytes << 28, bytes_accessed=megabytes << 20, transcendentals=megabytes << 18)


C_PACKETS, C_GIVE, C_PROJECT, C_AWAY, C_OWN, C_MIX = 1, 1, 2000, 4, 4, 2000
F32 = jnp.float32
BF16 = jnp.bfloat16


def silu(v):
    h = v * 0.5
    return h + h * jnp.tanh(h)


def layer_norm(values):
    mean = jnp.mean(values, axis=-1, keepdims=True)
    centred = values - mean
    var = jnp.mean(centred * centred, axis=-1, keepdims=True)
    return centred * lax.rsqrt(var + 1e-05)


def swap(value, axis):
    return lax.ppermute(value, axis, [(0, 1), (1, 0)])


def along(value, axis, steps):
    return lax.ppermute(value, axis, [(i, (i + steps) % 4) for i in range(4)])


def columns_kernel(in_ref, out_w_ref, out_ref, block, sems, out_sems):
    first = (lax.axis_index("x") * 2 + lax.axis_index("c")) * HEAD
    copies = []
    for part in range(5):
        ref, start = (in_ref, first + part * D) if part < 4 else (out_w_ref, first)
        at = pl.ds(pl.multiple_of(start, HEAD), HEAD)
        to = block.at[:, pl.ds(part * HEAD, HEAD)]
        copies.append(pltpu.make_async_copy(ref.at[:, at], to, sems.at[part]))
        copies[part].start()
    for copy in copies:
        copy.wait()
    copies = [pltpu.make_async_copy(block, out_ref.at[z], out_sems.at[z]) for z in range(8)]
    for copy in copies:
        copy.start()
    for copy in copies:
        copy.wait()


def columns(*args):
    return pl.pallas_call(
        columns_kernel,
        name="columns",
        out_shape=jax.ShapeDtypeStruct((8, 32, 640), BF16),
        in_specs=[ANY, ANY],
        out_specs=ANY,
        scratch_shapes=[
            pltpu.VMEM((32, 640), BF16),
            pltpu.SemaphoreType.DMA((5,)),
            pltpu.SemaphoreType.DMA((8,)),
        ],
        compiler_params=WHOLE,
    )(*args)


def tags_of(owner_ref, user, cutoff):
    square = (ROWS, ROWS)
    diagonal = lax.broadcasted_iota(jnp.int32, square, 0) == lax.broadcasted_iota(jnp.int32, square, 1)
    before = jnp.zeros(user.shape, jnp.int32)
    for b in range(32):
        before = before + (owner_ref[0, b] < user).astype(jnp.int32)

    def column(row):
        spread_out = jnp.where(diagonal, jnp.broadcast_to(row.astype(F32), square), 0.0)
        return jnp.sum(spread_out, axis=1, keepdims=True)

    lane = lax.broadcasted_iota(jnp.int32, (ROWS, 128), 1)
    tags = jnp.where(lane == 0, column(before), 0.0)
    tags = jnp.where(lane == 1, column(cutoff >> 6), tags)
    return jnp.where(lane == 2, column(cutoff & 63), tags)


def packets_kernel(place_ref, owner_ref, x_ref, user_ref, cutoff_ref, k_ref, v_ref, *out_refs):
    normed = layer_norm(x_ref[...].astype(F32)).astype(BF16)
    tags = tags_of(owner_ref, user_ref[...], cutoff_ref[...]).astype(BF16)
    for s, ref in enumerate(out_refs):
        for core in range(2):
            start = ((place_ref[0] + s) & 3) * 256 + core * HEAD
            at = pl.ds(pl.multiple_of(start, HEAD), HEAD)
            ref[core * 256 : core * 256 + 256, :] = k_ref[:, at]
            ref[512 + core * 256 : 768 + core * 256, :] = v_ref[:, at]
        for part in range(8):
            to = KV_ROWS + part * ROWS
            ref[to : to + ROWS, :] = normed[:, part * HEAD : part * HEAD + HEAD]
        ref[KV_ROWS + 512 :, :] = tags


def packets(*args):
    return pl.pallas_call(
        packets_kernel,
        name="packets",
        out_shape=[jax.ShapeDtypeStruct((KV_ROWS + MY_ROWS, HEAD), BF16)] * 4,
        in_specs=[SMEM, SMEM] + [VMEM] * 5,
        out_specs=[VMEM] * 4,
        cost_estimate=cost(C_PACKETS),
        compiler_params=PARAMS,
    )(*args)


def give_kernel(place_ref, p0, p1, p2, p3, rows_ref, more_ref, kv_ref):
    other = 1 - place_ref[1]
    for s, ref in enumerate((p0, p1, p2, p3)):
        for i in range(2):
            at = pl.ds(pl.multiple_of(i * 512 + other * 256, 256), 256)
            kv_ref[s * 512 + i * 256 : s * 512 + i * 256 + 256, :] = ref[at, :]
        to = (rows_ref, more_ref)[s // 2]
        to[(s % 2) * MY_ROWS : (s % 2 + 1) * MY_ROWS, :] = ref[KV_ROWS:, :]


def give(*args):
    return pl.pallas_call(
        give_kernel,
        name="give",
        out_shape=[jax.ShapeDtypeStruct((n, HEAD), BF16) for n in (2 * MY_ROWS, 2 * MY_ROWS, 2048)],
        in_specs=[SMEM] + [VMEM] * 4,
        out_specs=[VMEM] * 3,
        cost_estimate=cost(C_GIVE),
        compiler_params=PARAMS,
    )(*args)


def rows_kernel(p0, p1, p2, p3, got, more, rows):
    load_rows((p0, p1, p2, p3), (got, more), rows)


def assemble(*args):
    return pl.pallas_call(
        rows_kernel,
        name="assemble",
        out_shape=jax.ShapeDtypeStruct((HALF, WIDE), BF16),
        in_specs=[VMEM] * 6,
        out_specs=VMEM,
        compiler_params=PARAMS,
    )(*args)


def near_kernel(value_ref, after_ref, out_ref):
    out_ref[...] = value_ref[...]


def near(value, after):
    return pl.pallas_call(
        near_kernel,
        name="near",
        out_shape=jax.ShapeDtypeStruct(value.shape, value.dtype),
        in_specs=[VMEM, ANY],
        out_specs=VMEM,
        compiler_params=PARAMS,
    )(value, after)


def stack_kernel(*refs):
    for s in range(4):
        refs[-1][s] = refs[s][...]


def stack(first, *rest):
    return pl.pallas_call(
        stack_kernel,
        name="stack",
        out_shape=jax.ShapeDtypeStruct((4,) + first.shape, BF16),
        in_specs=[VMEM] * 4 + [ANY] * (len(rest) - 3),
        out_specs=VMEM,
        compiler_params=PARAMS,
    )(first, *rest)


def load_weight(place_ref, w_refs, w_all, first, count):
    for s, ref in enumerate(w_refs):
        y = (place_ref[3] - s + 4) & 3
        for z in range(8):
            at = pl.ds(pl.multiple_of(z * 128 + y * 32, 32), 32)
            w_all[at, :] = ref[pl.ds(z * 32, 32), pl.ds(first, count)]


def load_rows(packet_refs, got_refs, rows):
    for s in range(4):
        got = (got_refs[s // 2], (s % 2) * MY_ROWS)
        for rel, (ref, first) in enumerate(((packet_refs[s], KV_ROWS), got)):
            for part in range(9):
                to, start = rel * 256 + s * ROWS, first + part * ROWS
                rows[to : to + ROWS, pl.ds(part * HEAD, HEAD)] = ref[start : start + ROWS, :]


def visible(tags):
    return tags[:, 0:1] * BLOCK, tags[:, 1:2] * 64.0 + tags[:, 2:3]


def project_kernel(
    place_ref, w0, w1, w2, w3, rows, query_ref, gate_ref, den_ref, self_ref, part_ref, w_all
):
    for s, ref in enumerate((w0, w1, w2, w3)):
        part_ref[(place_ref[3] - s + 4) & 3] = ref[:, 512:]
    load_weight(place_ref, (w0, w1, w2, w3), w_all, 0, 512)
    for i in range(2):
        at = pl.ds(i * 256, 256)
        proj = jnp.dot(rows[at, :D], w_all[...], preferred_element_type=F32)
        proj = silu(proj).astype(BF16)
        gate_ref[at, :] = proj[:, 0:128]
        query_ref[at, :] = proj[:, 256:384]
        query = proj[:, 256:384].astype(F32)
        score = jnp.sum(query * proj[:, 384:512].astype(F32), axis=-1, keepdims=True)
        self_ref[at, :] = silu(score * SCALE) * proj[:, 128:256].astype(F32)
    labels = []
    for i in range(4):
        at = pl.ds(i * 128, 128)
        tags = rows[at, D:].astype(F32)
        first, last = visible(tags)
        den_ref[at, :] = jnp.broadcast_to(last - first + 1.0, (128, HEAD))
        labels.append(tags.T[0:4, :])
    query_ref[HALF:, :] = jnp.concatenate(labels, axis=0).astype(BF16)


def project(*args):
    shape = (HALF, HEAD)
    return pl.pallas_call(
        project_kernel,
        name="project",
        out_shape=[
            jax.ShapeDtypeStruct((HALF + 16, HEAD), BF16),
            jax.ShapeDtypeStruct(shape, BF16),
            jax.ShapeDtypeStruct(shape, F32),
            jax.ShapeDtypeStruct(shape, F32),
            jax.ShapeDtypeStruct((4, 256, HEAD), BF16),
        ],
        in_specs=[SMEM] + [VMEM] * 5,
        out_specs=[VMEM] * 5,
        scratch_shapes=[pltpu.VMEM((D, 512), BF16)],
        cost_estimate=cost(C_PROJECT),
        compiler_params=PARAMS,
    )(*args)


def attend_kernel(place_ref, q_ref, p0, p1, p2, p3, kv_peer, plus_ref, out_ref):
    x, core, half = place_ref[0], place_ref[1], place_ref[2]
    event = lax.broadcasted_iota(jnp.int32, (256, 256), 1)
    labels = q_ref[HALF : HALF + 16, :].astype(F32)
    for tile in range(2):
        at = pl.ds(tile * 256, 256)
        lows, counts = [], []
        for i in range(2):
            row = (tile * 2 + i) * 4
            tags = labels[row : row + 4, :]
            tags = jnp.concatenate([tags, jnp.zeros((124, 128), F32)], axis=0).T
            first, last = visible(tags)
            lows.append(first.astype(jnp.int32))
            counts.append((last - first).astype(jnp.uint32))
        low = jnp.broadcast_to(jnp.concatenate(lows, axis=0), (256, 256))
        count = jnp.broadcast_to(jnp.concatenate(counts, axis=0), (256, 256))
        query = q_ref[at, :]
        total = jnp.zeros((256, HEAD), F32)
        for rel in range(2):
            for s, pack in enumerate((p0, p1, p2, p3)):
                base = half * EVENTS + ((x - s + 4) & 3) * 512 + (core ^ rel) * 256
                row = s * 512 if rel else pl.multiple_of(core * 256, 256)
                keys, values = pl.ds(row, 256), pl.ds(row + (256 if rel else 512), 256)
                ref = kv_peer if rel else pack
                score = lax.dot_general(
                    query, ref[keys, :], (((1,), (1,)), ((), ())), preferred_element_type=F32
                )
                h = score * (0.5 * SCALE)
                w = h + h * jnp.tanh(h)
                seen = (event + base - low).astype(jnp.uint32) < count
                w = jnp.where(seen, w, 0.0).astype(BF16)
                total = total + jnp.dot(w, ref[values, :], preferred_element_type=F32)
        if out_ref.dtype == F32:
            total = total + plus_ref[at, :]
        out_ref[at, :] = total.astype(out_ref.dtype)


def attend(name, dtype, *args):
    return pl.pallas_call(
        attend_kernel,
        name=name,
        out_shape=jax.ShapeDtypeStruct((HALF, HEAD), dtype),
        in_specs=[SMEM] + [VMEM] * 7,
        out_specs=VMEM,
        cost_estimate=cost(C_AWAY if name == "other" else C_OWN),
        compiler_params=PARAMS,
    )(*args)


def mix_kernel(place_ref, sum_ref, home_ref, den_ref, gate_ref, out_ref):
    x, core = place_ref[0], place_ref[1]
    for rel in range(2):
        for s in range(4):
            at = pl.ds(rel * 256 + s * ROWS, ROWS)
            attended = (sum_ref[at, :] + home_ref[at, :].astype(F32)) / den_ref[at, :]
            mixed = layer_norm(attended) * gate_ref[at, :].astype(F32)
            out_ref[((x - s + 4) & 3) * 2 + (core ^ rel)] = mixed.astype(BF16)


def mix(*args):
    return pl.pallas_call(
        mix_kernel,
        name="mix",
        out_shape=jax.ShapeDtypeStruct((HEADS, ROWS, HEAD), BF16),
        in_specs=[SMEM] + [VMEM] * 4,
        out_specs=VMEM,
        cost_estimate=cost(C_MIX),
        compiler_params=PARAMS,
    )(*args)


def finish_kernel(place_ref, x_ref, mixed_ref, w0, w1, w2, w3, peer_ref, out_ref):
    along, core = place_ref[0], place_ref[1]
    pieces = [mixed_ref[h, :, y * 32 : y * 32 + 32] for y in range(4) for h in range(HEADS)]
    left = jnp.concatenate(pieces, axis=1)
    for s, ref in enumerate((w0, w1, w2, w3)):
        for rel in range(2):
            at = ((along - s + 4) & 3) * 2 + (core ^ rel)
            at = pl.ds(pl.multiple_of(at * HEAD, HEAD), HEAD)
            right = (ref[...] if rel == 0 else peer_ref[s]).reshape(D, HEAD)
            projected = jnp.dot(left, right, preferred_element_type=F32)
            out_ref[:, at] = (x_ref[:, at].astype(F32) + projected).astype(BF16)


def finish(*args):
    return pl.pallas_call(
        finish_kernel,
        name="finish",
        out_shape=jax.ShapeDtypeStruct((ROWS, D), BF16),
        in_specs=[SMEM] + [VMEM] * 7,
        out_specs=VMEM,
        compiler_params=PARAMS,
    )(*args)


def body(cand_embed, hist_key, hist_value, block_owner, cand_user, cand_cutoff, w_in, w_out):
    x = cand_embed[0]
    place = [lax.axis_index(a) for a in ("x", "c", "zh", "y")]
    place = jnp.stack(place).astype(jnp.int32)

    cols = columns(w_in, w_out)
    cols = lax.all_to_all(cols, "zl", 0, 0, tiled=True).reshape(256, 640)
    cols = [along(cols, "y", s) if s else cols for s in range(4)]

    packs = packets(place, block_owner, x, cand_user, cand_cutoff, hist_key[0], hist_value[0])
    packs = [along(pack, "x", s) if s else pack for s, pack in enumerate(packs)]
    got, more, kv_peer = [swap(part, "c") for part in give(place, *packs)]

    rows = assemble(*packs, got, more)
    query, gate, den, self_term, w_part = project(place, *cols, rows)
    query_other = swap(query, "zh")
    w_part = [along(w_part, "x", s) if s else w_part for s in range(4)]
    kv_peer = near(kv_peer, query)

    away = attend("other", BF16, place, query_other, *packs, kv_peer, self_term)
    home = swap(away, "zh")
    sums = attend("own", F32, place, query, *packs, kv_peer, self_term)
    w_own = stack(*w_part, away)
    w_peer = swap(w_own, "c")

    mixed = mix(place, sums, home, den, gate)
    mixed = lax.all_to_all(mixed, LOCAL, 0, 0, tiled=True)
    return finish(place, x, mixed, *w_part, w_peer)[None]


def solution(mesh):
    parts = Mesh(mesh.devices.reshape(2, 4, 2, 8, 4), ("zh", "x", "c", "zl", "y"))
    return jax.shard_map(
        body,
        mesh=parts,
        in_specs=(
            P(USER, HIST, None),
            P(USER, HIST, None),
            P(USER, HIST, None),
            P(USER, None),
            P(USER, HIST),
            P(USER, HIST),
            P(USER, None),
            P(USER, None),
        ),
        out_specs=P(USER, HIST, None),
        check_vma=False,
    )
```

```python
import jax
import jax.numpy as jnp
from jax import lax
from jax.experimental import pallas as pl
from jax.experimental.pallas import tpu as pltpu
from jax.sharding import Mesh, PartitionSpec as P

D = 1024
HEADS = 8
HEAD = 128
BLOCK = 128
ROWS = 64
WIDE = D + 128
KV_ROWS = 1024
MY_ROWS = 576
HALF = 512
EVENTS = 2048
USER = ("zl", "y")
LOCAL = ("x", "c")
HIST = ("zh", "x", "c")
SCALE = HEAD ** (-0.5)
VMEM = pl.BlockSpec(memory_space=pltpu.VMEM)
ANY = pl.BlockSpec(memory_space=pl.ANY)
SMEM = pl.BlockSpec(memory_space=pltpu.SMEM)
PARAMS = pltpu.CompilerParams(vmem_limit_bytes=16 << 20)
WHOLE = pltpu.CompilerParams(vmem_limit_bytes=60 << 20)

def cost(megabytes):
    return pl.CostEstimate(flops=megabytes << 28, bytes_accessed=megabytes << 20, transcendentals=megabytes << 18)


C_PACKETS, C_GIVE, C_PROJECT, C_AWAY, C_OWN, C_MIX = 1, 1, 2000, 4, 4, 2000
F32 = jnp.float32
BF16 = jnp.bfloat16


def silu(v):
    h = v * 0.5
    return h + h * jnp.tanh(h)


def layer_norm(values):
    mean = jnp.mean(values, axis=-1, keepdims=True)
    centred = values - mean
    var = jnp.mean(centred * centred, axis=-1, keepdims=True)
    return centred * lax.rsqrt(var + 1e-05)


def swap(value, axis):
    return lax.ppermute(value, axis, [(0, 1), (1, 0)])


def along(value, axis, steps):
    return lax.ppermute(value, axis, [(i, (i + steps) % 4) for i in range(4)])


def columns_kernel(in_ref, out_w_ref, out_ref, block, sems, out_sems):
    first = (lax.axis_index("x") * 2 + lax.axis_index("c")) * HEAD
    copies = []
    for part in range(5):
        ref, start = (in_ref, first + part * D) if part < 4 else (out_w_ref, first)
        at = pl.ds(pl.multiple_of(start, HEAD), HEAD)
        to = block.at[:, pl.ds(part * HEAD, HEAD)]
        copies.append(pltpu.make_async_copy(ref.at[:, at], to, sems.at[part]))
        copies[part].start()
    for copy in copies:
        copy.wait()
    copies = [pltpu.make_async_copy(block, out_ref.at[z], out_sems.at[z]) for z in range(8)]
    for copy in copies:
        copy.start()
    for copy in copies:
        copy.wait()


def columns(*args):
    return pl.pallas_call(
        columns_kernel,
        name="columns",
        out_shape=jax.ShapeDtypeStruct((8, 32, 640), BF16),
        in_specs=[ANY, ANY],
        out_specs=ANY,
        scratch_shapes=[
            pltpu.VMEM((32, 640), BF16),
            pltpu.SemaphoreType.DMA((5,)),
            pltpu.SemaphoreType.DMA((8,)),
        ],
        compiler_params=WHOLE,
    )(*args)


def tags_of(owner_ref, user, cutoff):
    square = (ROWS, ROWS)
    diagonal = lax.broadcasted_iota(jnp.int32, square, 0) == lax.broadcasted_iota(jnp.int32, square, 1)
    before = jnp.zeros(user.shape, jnp.int32)
    for b in range(32):
        before = before + (owner_ref[0, b] < user).astype(jnp.int32)

    def column(row):
        spread_out = jnp.where(diagonal, jnp.broadcast_to(row.astype(F32), square), 0.0)
        return jnp.sum(spread_out, axis=1, keepdims=True)

    lane = lax.broadcasted_iota(jnp.int32, (ROWS, 128), 1)
    tags = jnp.where(lane == 0, column(before), 0.0)
    tags = jnp.where(lane == 1, column(cutoff >> 6), tags)
    return jnp.where(lane == 2, column(cutoff & 63), tags)


def packets_kernel(place_ref, owner_ref, x_ref, user_ref, cutoff_ref, k_ref, v_ref, *out_refs):
    normed = layer_norm(x_ref[...].astype(F32)).astype(BF16)
    tags = tags_of(owner_ref, user_ref[...], cutoff_ref[...]).astype(BF16)
    for s, ref in enumerate(out_refs):
        for core in range(2):
            start = ((place_ref[0] + s) & 3) * 256 + core * HEAD
            at = pl.ds(pl.multiple_of(start, HEAD), HEAD)
            ref[core * 256 : core * 256 + 256, :] = k_ref[:, at]
            ref[512 + core * 256 : 768 + core * 256, :] = v_ref[:, at]
        for part in range(8):
            to = KV_ROWS + part * ROWS
            ref[to : to + ROWS, :] = normed[:, part * HEAD : part * HEAD + HEAD]
        ref[KV_ROWS + 512 :, :] = tags


def packets(*args):
    return pl.pallas_call(
        packets_kernel,
        name="packets",
        out_shape=[jax.ShapeDtypeStruct((KV_ROWS + MY_ROWS, HEAD), BF16)] * 4,
        in_specs=[SMEM, SMEM] + [VMEM] * 5,
        out_specs=[VMEM] * 4,
        cost_estimate=cost(C_PACKETS),
        compiler_params=PARAMS,
    )(*args)


def give_kernel(place_ref, p0, p1, p2, p3, rows_ref, more_ref, kv_ref):
    other = 1 - place_ref[1]
    for s, ref in enumerate((p0, p1, p2, p3)):
        for i in range(2):
            at = pl.ds(pl.multiple_of(i * 512 + other * 256, 256), 256)
            kv_ref[s * 512 + i * 256 : s * 512 + i * 256 + 256, :] = ref[at, :]
        to = (rows_ref, more_ref)[s // 2]
        to[(s % 2) * MY_ROWS : (s % 2 + 1) * MY_ROWS, :] = ref[KV_ROWS:, :]


def give(*args):
    return pl.pallas_call(
        give_kernel,
        name="give",
        out_shape=[jax.ShapeDtypeStruct((n, HEAD), BF16) for n in (2 * MY_ROWS, 2 * MY_ROWS, 2048)],
        in_specs=[SMEM] + [VMEM] * 4,
        out_specs=[VMEM] * 3,
        cost_estimate=cost(C_GIVE),
        compiler_params=PARAMS,
    )(*args)


def rows_kernel(p0, p1, p2, p3, got, more, rows):
    load_rows((p0, p1, p2, p3), (got, more), rows)


def assemble(*args):
    return pl.pallas_call(
        rows_kernel,
        name="assemble",
        out_shape=jax.ShapeDtypeStruct((HALF, WIDE), BF16),
        in_specs=[VMEM] * 6,
        out_specs=VMEM,
        compiler_params=PARAMS,
    )(*args)


def near_kernel(value_ref, after_ref, out_ref):
    out_ref[...] = value_ref[...]


def near(value, after):
    return pl.pallas_call(
        near_kernel,
        name="near",
        out_shape=jax.ShapeDtypeStruct(value.shape, value.dtype),
        in_specs=[VMEM, ANY],
        out_specs=VMEM,
        compiler_params=PARAMS,
    )(value, after)


def stack_kernel(*refs):
    for s in range(4):
        refs[-1][s] = refs[s][...]


def stack(first, *rest):
    return pl.pallas_call(
        stack_kernel,
        name="stack",
        out_shape=jax.ShapeDtypeStruct((4,) + first.shape, BF16),
        in_specs=[VMEM] * 4 + [ANY] * (len(rest) - 3),
        out_specs=VMEM,
        compiler_params=PARAMS,
    )(first, *rest)


def load_weight(place_ref, w_refs, w_all, first, count):
    for s, ref in enumerate(w_refs):
        y = (place_ref[3] - s + 4) & 3
        for z in range(8):
            at = pl.ds(pl.multiple_of(z * 128 + y * 32, 32), 32)
            w_all[at, :] = ref[pl.ds(z * 32, 32), pl.ds(first, count)]


def load_rows(packet_refs, got_refs, rows):
    for s in range(4):
        got = (got_refs[s // 2], (s % 2) * MY_ROWS)
        for rel, (ref, first) in enumerate(((packet_refs[s], KV_ROWS), got)):
            for part in range(9):
                to, start = rel * 256 + s * ROWS, first + part * ROWS
                rows[to : to + ROWS, pl.ds(part * HEAD, HEAD)] = ref[start : start + ROWS, :]


def visible(tags):
    return tags[:, 0:1] * BLOCK, tags[:, 1:2] * 64.0 + tags[:, 2:3]


def project_kernel(place_ref, w0, w1, w2, w3, rows, query_ref, part_ref, w_all):
    load_weight(place_ref, (w0, w1, w2, w3), w_all, 256, HEAD)
    query = jnp.dot(rows[:, :D], w_all[...], preferred_element_type=F32)
    query_ref[0:HALF, :] = silu(query).astype(BF16)
    labels = [rows[i * 128 : i * 128 + 128, D:].astype(F32).T[0:4, :] for i in range(4)]
    query_ref[HALF:, :] = jnp.concatenate(labels, axis=0).astype(BF16)
    for s, ref in enumerate((w0, w1, w2, w3)):
        part_ref[(place_ref[3] - s + 4) & 3] = ref[:, 512:]


def project(*args):
    return pl.pallas_call(
        project_kernel,
        name="project",
        out_shape=[
            jax.ShapeDtypeStruct((HALF + 16, HEAD), BF16),
            jax.ShapeDtypeStruct((4, 256, HEAD), BF16),
        ],
        in_specs=[SMEM] + [VMEM] * 5,
        out_specs=[VMEM] * 2,
        scratch_shapes=[pltpu.VMEM((D, HEAD), BF16)],
        cost_estimate=cost(C_PROJECT),
        compiler_params=PARAMS,
    )(*args)


def gates_kernel(place_ref, w0, w1, w2, w3, rows, query_ref, gate_ref, den_ref, self_ref, w_all):
    for first, to in ((0, 0), (384, 256)):
        count = 256 if first == 0 else 128
        for s, ref in enumerate((w0, w1, w2, w3)):
            y = (place_ref[3] - s + 4) & 3
            for z in range(8):
                at = pl.ds(pl.multiple_of(z * 128 + y * 32, 32), 32)
                w_all[at, to : to + count] = ref[pl.ds(z * 32, 32), first : first + count]
    for i in range(2):
        at = pl.ds(i * 256, 256)
        proj = jnp.dot(rows[at, :D], w_all[...], preferred_element_type=F32)
        proj = silu(proj).astype(BF16)
        gate_ref[at, :] = proj[:, 0:128]
        query = query_ref[at, :].astype(F32)
        score = jnp.sum(query * proj[:, 256:384].astype(F32), axis=-1, keepdims=True)
        self_ref[at, :] = silu(score * SCALE) * proj[:, 128:256].astype(F32)
        first, last = visible(rows[at, D:].astype(F32))
        den_ref[at, :] = jnp.broadcast_to(last - first + 1.0, (256, HEAD))


def gates(*args):
    shape = (HALF, HEAD)
    return pl.pallas_call(
        gates_kernel,
        name="gates",
        out_shape=[jax.ShapeDtypeStruct(shape, t) for t in (BF16, F32, F32)],
        in_specs=[SMEM] + [VMEM] * 6,
        out_specs=[VMEM] * 3,
        scratch_shapes=[pltpu.VMEM((D, 384), BF16)],
        cost_estimate=cost(C_OWN),
        compiler_params=PARAMS,
    )(*args)


def attend_kernel(place_ref, q_ref, p0, p1, p2, p3, kv_peer, plus_ref, out_ref):
    x, core, half = place_ref[0], place_ref[1], place_ref[2]
    event = lax.broadcasted_iota(jnp.int32, (256, 256), 1)
    labels = q_ref[HALF : HALF + 16, :].astype(F32)
    for tile in range(2):
        at = pl.ds(tile * 256, 256)
        lows, counts = [], []
        for i in range(2):
            row = (tile * 2 + i) * 4
            tags = labels[row : row + 4, :]
            tags = jnp.concatenate([tags, jnp.zeros((124, 128), F32)], axis=0).T
            first, last = visible(tags)
            lows.append(first.astype(jnp.int32))
            counts.append((last - first).astype(jnp.uint32))
        low = jnp.broadcast_to(jnp.concatenate(lows, axis=0), (256, 256))
        count = jnp.broadcast_to(jnp.concatenate(counts, axis=0), (256, 256))
        query = q_ref[at, :]
        total = jnp.zeros((256, HEAD), F32)
        for rel in range(2):
            for s, pack in enumerate((p0, p1, p2, p3)):
                base = half * EVENTS + ((x - s + 4) & 3) * 512 + (core ^ rel) * 256
                row = s * 512 if rel else pl.multiple_of(core * 256, 256)
                keys, values = pl.ds(row, 256), pl.ds(row + (256 if rel else 512), 256)
                ref = kv_peer if rel else pack
                score = lax.dot_general(
                    query, ref[keys, :], (((1,), (1,)), ((), ())), preferred_element_type=F32
                )
                h = score * (0.5 * SCALE)
                w = h + h * jnp.tanh(h)
                seen = (event + base - low).astype(jnp.uint32) < count
                w = jnp.where(seen, w, 0.0).astype(BF16)
                total = total + jnp.dot(w, ref[values, :], preferred_element_type=F32)
        if out_ref.dtype == F32:
            total = total + plus_ref[at, :]
        out_ref[at, :] = total.astype(out_ref.dtype)


def attend(name, dtype, *args):
    return pl.pallas_call(
        attend_kernel,
        name=name,
        out_shape=jax.ShapeDtypeStruct((HALF, HEAD), dtype),
        in_specs=[SMEM] + [VMEM] * 7,
        out_specs=VMEM,
        cost_estimate=cost(C_AWAY if name == "other" else C_OWN),
        compiler_params=PARAMS,
    )(*args)


def mix_kernel(place_ref, sum_ref, home_ref, den_ref, gate_ref, out_ref):
    x, core = place_ref[0], place_ref[1]
    for rel in range(2):
        for s in range(4):
            at = pl.ds(rel * 256 + s * ROWS, ROWS)
            attended = (sum_ref[at, :] + home_ref[at, :].astype(F32)) / den_ref[at, :]
            mixed = layer_norm(attended) * gate_ref[at, :].astype(F32)
            out_ref[((x - s + 4) & 3) * 2 + (core ^ rel)] = mixed.astype(BF16)


def mix(*args):
    return pl.pallas_call(
        mix_kernel,
        name="mix",
        out_shape=jax.ShapeDtypeStruct((HEADS, ROWS, HEAD), BF16),
        in_specs=[SMEM] + [VMEM] * 4,
        out_specs=VMEM,
        cost_estimate=cost(C_MIX),
        compiler_params=PARAMS,
    )(*args)


def finish_kernel(place_ref, x_ref, mixed_ref, w0, w1, w2, w3, peer_ref, out_ref):
    along, core = place_ref[0], place_ref[1]
    pieces = [mixed_ref[h, :, y * 32 : y * 32 + 32] for y in range(4) for h in range(HEADS)]
    left = jnp.concatenate(pieces, axis=1)
    for s, ref in enumerate((w0, w1, w2, w3)):
        for rel in range(2):
            at = ((along - s + 4) & 3) * 2 + (core ^ rel)
            at = pl.ds(pl.multiple_of(at * HEAD, HEAD), HEAD)
            right = (ref[...] if rel == 0 else peer_ref[s]).reshape(D, HEAD)
            projected = jnp.dot(left, right, preferred_element_type=F32)
            out_ref[:, at] = (x_ref[:, at].astype(F32) + projected).astype(BF16)


def finish(*args):
    return pl.pallas_call(
        finish_kernel,
        name="finish",
        out_shape=jax.ShapeDtypeStruct((ROWS, D), BF16),
        in_specs=[SMEM] + [VMEM] * 7,
        out_specs=VMEM,
        compiler_params=PARAMS,
    )(*args)


def body(cand_embed, hist_key, hist_value, block_owner, cand_user, cand_cutoff, w_in, w_out):
    x = cand_embed[0]
    place = [lax.axis_index(a) for a in ("x", "c", "zh", "y")]
    place = jnp.stack(place).astype(jnp.int32)

    cols = columns(w_in, w_out)
    cols = lax.all_to_all(cols, "zl", 0, 0, tiled=True).reshape(256, 640)
    cols = [along(cols, "y", s) if s else cols for s in range(4)]

    packs = packets(place, block_owner, x, cand_user, cand_cutoff, hist_key[0], hist_value[0])
    packs = [along(pack, "x", s) if s else pack for s, pack in enumerate(packs)]
    got, more, kv_peer = [swap(part, "c") for part in give(place, *packs)]

    rows = assemble(*packs, got, more)
    query, w_part = project(place, *cols, rows)
    gate, den, self_term = gates(place, *cols, rows, query)
    query_other = swap(query, "zh")
    w_part = [along(w_part, "x", s) if s else w_part for s in range(4)]
    kv_peer = near(kv_peer, query)

    away = attend("other", BF16, place, query_other, *packs, kv_peer, query_other)
    home = swap(away, "zh")
    sums = attend("own", F32, place, query, *packs, kv_peer, self_term)
    w_own = stack(*w_part, away)
    w_peer = swap(w_own, "c")

    mixed = mix(place, sums, home, den, gate)
    mixed = lax.all_to_all(mixed, LOCAL, 0, 0, tiled=True)
    return finish(place, x, mixed, *w_part, w_peer)[None]


def solution(mesh):
    parts = Mesh(mesh.devices.reshape(2, 4, 2, 8, 4), ("zh", "x", "c", "zl", "y"))
    return jax.shard_map(
        body,
        mesh=parts,
        in_specs=(
            P(USER, HIST, None),
            P(USER, HIST, None),
            P(USER, HIST, None),
            P(USER, None),
            P(USER, HIST),
            P(USER, HIST),
            P(USER, None),
            P(USER, None),
        ),
        out_specs=P(USER, HIST, None),
        check_vma=False,
    )
```
